32 devices in a mesh: leaf: 8 (over z, y), rhs: 4 (over x, core).
Axes of the slice: x: 2, y: 2, z: 4, core: 2. Of those that a mesh axis runs over, the one named last changes fastest.
Arguments:
- rhs_in: float32 [16384, 512], P(('leaf', 'rhs')), may hold values from -6 to 6
- rhs_top: float32 [896, 512], P(None, 'rhs'), may hold values from -6 to 6
- leaf_inv: float32 [32, 512, 512], P('leaf')
- leaf_coupling: float32 [32, 384, 512], P('leaf'), may hold values from -0.125 to 0.125
- coupling_rows: int32 [32, 384], P('leaf'), may hold values from 0 to 383, each once within a row
- top_inv: float32 [7, 128, 128], replicated
- top_coupling: float32 [10, 128, 128], replicated, may hold values from -0.25 to 0.25
Outputs:
- solution_leaf: float32 [16384, 512], P(('leaf', 'rhs'))
- solution_top: float32 [896, 512], P(None, 'rhs')
The draws below stay inside these ranges and needn't reach their ends.
All inputs are finite; a program needn't handle non-finite values.
Results may differ from the reference program's by a relative error of at most 0.0003.
Values sent between devices are 32-bit elements; how exact they have to be, the bound alone decides.
No kernel may reach another device: no remote copies, remote signals or barrier semaphores. Data moves between devices by JAX's collectives and lax.ppermute only.
A program may use at most 64 MiB of HBM per device.

```python
import jax
import jax.numpy as jnp
from jax import lax

PW = 128
LEV = 3
S = 512
NB = 4
NRHS = 512
NP = 7
NTOP = 896
LP = 384
NPAIRS = 10
LEAFBLOCKS = 32
CELLS = 16384
N_LEAF = 8


def triangle(key, count, order, low, high):
    first, second = jax.random.split(key)
    diagonal = jnp.exp(jax.random.uniform(first, (count, order), jnp.float32, jnp.log(low), jnp.log(high)))
    spread = jax.random.normal(second, (count, order, order), jnp.float32) * (0.6 / order ** 0.5)
    rowsidx = jnp.arange(order)[:, None]
    colsidx = jnp.arange(order)[None, :]
    lower = (rowsidx > colsidx)[None, :, :]
    unit = (rowsidx == colsidx)[None, :, :]
    return jnp.where(lower, spread, 0.0) + jnp.where(unit, diagonal[:, :, None], 0.0)


def draw_leaf_inv(key, part):
    return triangle(key, LEAFBLOCKS, S, 1.0, 2.0)


def draw_top_inv(key, part):
    return triangle(key, NP, PW, 1.0, 2.0)


def block_levels(stream_key, extent, cuts, smallest, high):
    def one(axis_at, shards_of):
        steps = jax.random.uniform(jax.random.fold_in(jax.random.fold_in(stream_key, 6), axis_at), (shards_of,), jnp.float32, smallest / len(cuts), high / len(cuts))
        return jnp.repeat(jnp.exp(steps), extent[axis_at] // shards_of).reshape((-1,) + (1,) * (len(extent) - axis_at - 1))

    factor_of = one(*cuts[0])
    for cut in cuts[1:]:
        factor_of = factor_of * one(*cut)
    return factor_of


def bell_draw(rng, extent, scale, reach, cuts=(), held_as=jnp.bfloat16):
    entries = scale * jax.random.normal(rng, extent, jnp.float32)
    if cuts:
        entries = entries * block_levels(rng, extent, cuts, -0.22, 0.18)
    return jnp.clip(entries, -reach, reach).astype(held_as)


def setup_inputs(seed: int = 0) -> dict:
    key_of = jax.random.split(jax.random.key(seed), 8)
    rhs_in = bell_draw(key_of[0], (CELLS, NRHS), 1.0, 6.0, ((0, 32),), jnp.float32)
    rhs_top = bell_draw(key_of[1], (NTOP, NRHS), 1.0, 6.0, ((1, 4),), jnp.float32)
    leaf_inv = draw_leaf_inv(jax.random.fold_in(key_of[7], 71), 0)
    leaf_coupling = bell_draw(key_of[3], (LEAFBLOCKS, LP, S), (4 * S) ** -0.5, 0.125, ((0, 8),), jnp.float32)
    coupling_rows = jax.vmap(lambda own: jax.random.permutation(own, LP))(jax.random.split(key_of[4], LEAFBLOCKS)).reshape((LEAFBLOCKS, LP)).astype(jnp.int32)
    top_inv = draw_top_inv(jax.random.fold_in(key_of[7], 71), 0)
    top_coupling = bell_draw(key_of[6], (NPAIRS, PW, PW), (4 * PW) ** -0.5, 0.25, (), jnp.float32)
    return dict(rhs_in=rhs_in, rhs_top=rhs_top, leaf_inv=leaf_inv, leaf_coupling=leaf_coupling, coupling_rows=coupling_rows, top_inv=top_inv, top_coupling=top_coupling)


highest = lax.Precision.HIGHEST


def matmul(left, right):
    return jnp.dot(left, right, precision=highest, preferred_element_type=jnp.float32)


def ancestor_pairs(levels):
    pairs = []
    for panel in range(1, 2 ** levels - 1):
        above = panel
        while above > 0:
            above = (above - 1) // 2
            pairs.append((panel, above))
    return pairs


def top_solve(rhs_panels, top_inv, top_coupling, levels):
    panel_count = 2 ** levels - 1
    pairs = ancestor_pairs(levels)
    forward = [None] * panel_count
    for panel in reversed(range(panel_count)):
        accum = rhs_panels[panel]
        for number, (below, above) in enumerate(pairs):
            if above == panel:
                accum = accum - matmul(top_coupling[number], forward[below])
        forward[panel] = matmul(top_inv[panel], accum)
    result = [None] * panel_count
    for panel in range(panel_count):
        accum = forward[panel]
        for number, (below, above) in enumerate(pairs):
            if below == panel:
                accum = accum - matmul(top_coupling[number].T, result[above])
        result[panel] = matmul(top_inv[panel].T, accum)
    return jnp.stack(result)


def path_index(device, levels, leaf_count, width):
    panel = 2 ** (levels - 1) - 1 + device * 2 ** (levels - 1) // leaf_count
    pieces = []
    for level in range(levels):
        pieces.append(panel * width + jnp.arange(width, dtype=jnp.int32))
        panel = (panel - 1) // 2
    return jnp.concatenate(pieces).astype(jnp.int32)


def reference(rhs_in, rhs_top, leaf_inv, leaf_coupling, coupling_rows, top_inv, top_coupling):
    blocks = rhs_in.reshape(LEAFBLOCKS, S, NRHS)
    numbers = jnp.arange(LEAFBLOCKS, dtype=jnp.int32)

    def forward_block(carry, item):
        number, rhs_block, inverse, coupling, rows = item
        lifted_block = matmul(inverse, rhs_block)
        target = path_index(number // NB, LEV, N_LEAF, PW)[rows]
        return carry.at[target].add(matmul(coupling, lifted_block)), lifted_block

    start = jnp.zeros((NTOP, NRHS), jnp.float32)
    total, lifted = lax.scan(forward_block, start, (numbers, blocks, leaf_inv, leaf_coupling, coupling_rows))
    top_rhs = rhs_top - total
    solution_top = top_solve(top_rhs.reshape(NP, PW, NRHS), top_inv, top_coupling, LEV).reshape(NTOP, NRHS)

    def backward_block(item):
        number, lifted_block, inverse, coupling, rows = item
        target = path_index(number // NB, LEV, N_LEAF, PW)[rows]
        picked = solution_top[target]
        return matmul(inverse.T, lifted_block - matmul(coupling.T, picked))

    solution_leaf = lax.map(backward_block, (numbers, lifted, leaf_inv, leaf_coupling, coupling_rows))
    return solution_leaf.reshape(CELLS, NRHS), solution_top
```

```python
import jax
import jax.numpy as jnp
from jax import lax
from jax.sharding import PartitionSpec as P

high = lax.Precision.HIGH


def dot(left, right, dims):
    return lax.dot_general(
        left, right, (dims, ((), ())), precision=high, preferred_element_type=jnp.float32
    )


def nn(left, right):
    return dot(left, right, ((1,), (0,)))


def tn(left, right):
    return dot(left, right, ((0,), (0,)))


def swap(value, axis_sizes, partner):
    leaf_count, group_count = axis_sizes
    pairs = []
    for leaf in range(leaf_count):
        for group in range(group_count):
            to_leaf, to_group = partner(leaf, group)
            pairs.append((leaf * group_count + group, to_leaf * group_count + to_group))
    return lax.ppermute(value, ("leaf", "rhs"), pairs)


def per_device(rhs_in, rhs_top, leaf_inv, leaf_coupling, coupling_rows, top_inv, top_coupling):
    block_count, order, _ = leaf_inv.shape
    panel_count, width, _ = top_inv.shape
    levels = (panel_count + 1).bit_length() - 1
    columns = rhs_top.shape[1]
    path_length = coupling_rows.shape[1]
    leaf_count = lax.axis_size("leaf")
    group_count = lax.axis_size("rhs")
    sizes = (leaf_count, group_count)
    leaf = lax.axis_index("leaf")
    group = lax.axis_index("rhs")
    bottoms = 2 ** (levels - 1)
    sharers = leaf_count // bottoms
    place = leaf // sharers
    core, half = group % 2, group // 2
    keep = jnp.where(core == 0, half, leaf % 2)

    def flip_first(lf, gr):
        return (lf, gr ^ 2) if gr % 2 == 0 else (lf ^ 1, gr)

    def flip_second(lf, gr):
        return (lf ^ 1, gr) if gr % 2 == 0 else (lf, gr ^ 2)

    path = [bottoms - 1 + place]
    for level in range(1, levels):
        path.append((path[-1] - 1) // 2)
    first_pair = []
    for level in range(levels):
        depth = levels - 1 - level
        before = sum(d * 2**d for d in range(depth))
        first_pair.append(before + (path[level] - (2**depth - 1)) * depth)
    inv = [lax.dynamic_index_in_dim(top_inv, path[level], 0, False) for level in range(levels)]
    coup = {}
    for below in range(levels):
        for above in range(below + 1, levels):
            coup[below, above] = lax.dynamic_index_in_dim(
                top_coupling, first_pair[below] + above - below - 1, 0, False
            )

    per_group = block_count // group_count
    first = group * per_group
    panels = rhs_top.reshape(panel_count, width, columns)
    total = None
    lifted_all, coupling_all, inv_all = [], [], []
    for block in range(per_group):
        my_inv = lax.dynamic_index_in_dim(leaf_inv, first + block, 0, False)
        my_coupling = lax.dynamic_index_in_dim(leaf_coupling, first + block, 0, False)
        my_rows = lax.dynamic_index_in_dim(coupling_rows, first + block, 0, False)
        chosen = (jnp.arange(path_length)[:, None] == my_rows[None, :]).astype(jnp.float32)
        permuted = nn(chosen, my_coupling)
        lifted = nn(my_inv, rhs_in[block * order : (block + 1) * order])
        terms = nn(permuted, lifted)
        total = terms if total is None else total + terms
        lifted_all.append(lifted)
        coupling_all.append(permuted)
        inv_all.append(my_inv)
    total = total.reshape(path_length, 2, 2, columns)
    other = lax.dynamic_index_in_dim(total, 1 - core, 2, False).transpose(1, 0, 2)
    mine = lax.dynamic_index_in_dim(total, core, 2, False).transpose(1, 0, 2)
    base = []
    for level in range(levels):
        counts = (leaf % (sharers * 2**level)) == 0
        rows = lax.dynamic_index_in_dim(panels, path[level], 0, False)
        base.append(jnp.where(counts, rows, 0.0))
    base = jnp.concatenate(base, 0)
    got = swap(other, sizes, lambda lf, gr: (lf, gr ^ 1))
    number = jnp.arange(2)[:, None, None]
    mine = jnp.where(number == half, base[None], 0.0) - mine - got
    got = swap(lax.dynamic_index_in_dim(mine, 1 - keep, 0, False), sizes, flip_first)
    value = lax.dynamic_index_in_dim(mine, keep, 0, False) + got
    value = value + swap(value, sizes, flip_second)
    bit = 2
    while bit < sharers:
        value = value + swap(value, sizes, lambda lf, gr, bit=bit: (lf ^ bit, gr))
        bit *= 2

    forward = []
    rows = [value[level * width : (level + 1) * width] for level in range(levels)]
    for level in range(levels):
        forward.append(nn(inv[level], rows[level]))
        if level + 1 < levels:
            rest = jnp.concatenate(
                [rows[above] - nn(coup[level, above], forward[level]) for above in range(level + 1, levels)], 0
            )
            bit = sharers * 2**level
            rest = rest + swap(rest, sizes, lambda lf, gr, bit=bit: (lf ^ bit, gr))
            for above in range(level + 1, levels):
                rows[above] = rest[(above - level - 1) * width : (above - level) * width]
    solved = [None] * levels
    for level in reversed(range(levels)):
        accum = forward[level]
        for above in reversed(range(level + 1, levels)):
            accum = accum - tn(coup[level, above], solved[above])
        solved[level] = tn(inv[level], accum)
    solved = jnp.concatenate(solved, 0)

    got = swap(solved, sizes, flip_first)
    pair = jnp.where((number == keep), solved[None], got[None])
    got = swap(pair, sizes, lambda lf, gr: (lf, gr ^ 1))
    core_number = jnp.arange(2)[None, :, None, None]
    full = jnp.where(core_number == core, pair[:, None], got[:, None])
    full = full.transpose(2, 0, 1, 3).reshape(path_length, group_count * columns)
    answers = []
    for block in range(per_group):
        inner = lifted_all[block] - tn(coupling_all[block], full)
        answers.append(tn(inv_all[block], inner))

    own = lax.dynamic_index_in_dim(pair, half, 0, False)
    depths = {levels - 1: own[None, :width]}
    for level in range(1, levels):
        bit = sharers * 2 ** (level - 1)
        sent = jnp.concatenate([depths[d] for d in sorted(depths)], 0)
        came = swap(sent, sizes, lambda lf, gr, bit=bit: (lf ^ bit, gr))
        late = (leaf // bit) % 2
        offset = 0
        for d in sorted(depths):
            count = depths[d].shape[0]
            theirs = came[offset : offset + count]
            offset += count
            depths[d] = jnp.where(
                late == 1,
                jnp.concatenate([theirs, depths[d]], 0),
                jnp.concatenate([depths[d], theirs], 0),
            )
        depths[levels - 1 - level] = own[None, level * width : (level + 1) * width]
    top = jnp.concatenate([depths[d] for d in sorted(depths)], 0)
    return jnp.concatenate(answers, 0), top.reshape(panel_count * width, columns)


def solution(mesh):
    placed = (
        P(("leaf", "rhs"), None),
        P(None, "rhs"),
        P("leaf", None, None),
        P("leaf", None, None),
        P("leaf", None),
        P(),
        P(),
    )
    return jax.shard_map(
        per_device,
        mesh=mesh,
        in_specs=placed,
        out_specs=(P(("leaf", "rhs"), None), P(None, "rhs")),
        check_vma=False,
    )
```

```python
import functools

import jax
import jax.numpy as jnp
from jax import lax
from jax.experimental import pallas as pl
from jax.experimental.pallas import tpu as pltpu
from jax.sharding import PartitionSpec as P

F32, BF16 = jnp.float32, jnp.bfloat16
high = lax.Precision.HIGH


def dot(left, right):
    return jnp.dot(left, right, preferred_element_type=F32)


def dot_high(left, right):
    return jnp.dot(left, right, precision=high, preferred_element_type=F32)


def split(value):
    hi = value.astype(BF16)
    return hi, (value - hi.astype(F32)).astype(BF16)


def dot_split(left_hi, left_lo, right):
    hi, lo = split(right)
    return dot(left_hi, hi) + (dot(left_hi, lo) + dot(left_lo, hi))


def lanes(number, width):
    return pl.ds(pl.multiple_of(number * width, width), width)


class Plan:
    def __init__(self, leaf_count, group_count, panel_count, width):
        self.width = width
        self.levels = (panel_count + 1).bit_length() - 1
        self.bottoms = 2 ** (self.levels - 1)
        self.leaf_count, self.group_count = leaf_count, group_count
        self.sharers = leaf_count // self.bottoms

    def here(self):
        leaf, group = lax.axis_index("leaf"), lax.axis_index("rhs")
        return leaf, leaf // self.sharers, group % 2, group // 2

    def panel(self, place, level, flip=0):
        depth = self.levels - 1 - level
        return 2**depth - 1 + ((place >> level) ^ flip)

    def pair(self, place, below, above, flip=0):
        depth = self.levels - 1 - below
        before = sum(d * 2**d for d in range(depth))
        return before + ((place >> below) ^ flip) * depth + (above - below - 1)

    def swap(self, value, partner):
        pairs = []
        for leaf in range(self.leaf_count):
            for group in range(self.group_count):
                to_leaf, to_group = partner(leaf, group)
                pairs.append((leaf * self.group_count + group, to_leaf * self.group_count + to_group))
        return lax.ppermute(value, ("leaf", "rhs"), pairs)

    def swap_rhs(self, value, bit):
        return self.swap(value, lambda leaf, group: (leaf, group ^ bit))

    def swap_leaf(self, value, bit):
        return self.swap(value, lambda leaf, group: (leaf ^ bit, group))


def lift_kernel(plan, order, width, rhs, inv, coupling, rows, sent, rhs_own, lifted, inv_hi, inv_lo,
                perm_hi, perm_lo, rhs_buf, inv_buf, coup_buf, row_buf, sems):
    _, _, core, half = plan.here()
    block = half * 2 + core
    path = coupling.shape[1]
    copies = [
        pltpu.make_async_copy(rows.at[pl.ds(block, 1)], row_buf, sems.at[0]),
        pltpu.make_async_copy(coupling.at[block], coup_buf, sems.at[1]),
    ]
    for number, side in enumerate((1 - half, half)):
        copies.append(pltpu.make_async_copy(
            rhs.at[:, lanes(side * 2 + 1 - core, width)],
            rhs_buf.at[:, pl.ds(number * width, width)], sems.at[2 + number]))
    copies.append(pltpu.make_async_copy(inv.at[block], inv_buf, sems.at[4]))
    for number, side in enumerate((1 - half, half)):
        copies.append(pltpu.make_async_copy(
            rhs.at[:, lanes(side * 2 + core, width)],
            rhs_own.at[:, pl.ds(number * width, width)], sems.at[5 + number]))
    for copy in copies:
        copy.start()
    copies[0].wait()
    chosen = (lax.broadcasted_iota(jnp.int32, (path, path), 0) == row_buf[...]).astype(BF16)
    copies[1].wait()
    coup_hi, coup_lo = split(coup_buf[...])
    perm_hi[...] = dot(chosen, coup_hi).astype(BF16)
    perm_lo[...] = dot(chosen, coup_lo).astype(BF16)
    copies[2].wait()
    copies[3].wait()
    copies[4].wait()
    hi, lo = split(inv_buf[...])
    inv_hi[...] = hi
    inv_lo[...] = lo
    result = dot_split(hi, lo, rhs_buf[...])
    lifted[...] = result
    terms = dot_split(perm_hi[...], perm_lo[...], result)
    sent[0] = -terms[:, :width]
    sent[1] = -terms[:, width:]
    copies[5].wait()
    copies[6].wait()


def own_kernel(plan, width, rhs_own, inv_hi, inv_lo, perm_hi, perm_lo, top, own, lifted):
    leaf, place, _, _ = plan.here()
    result = dot_split(inv_hi[...], inv_lo[...], rhs_own[...])
    lifted[...] = result
    terms = dot_split(perm_hi[...], perm_lo[...], result)
    own[0] = -terms[:, :width]
    for level in range(plan.levels):
        rows = pl.ds(level * plan.width, plan.width)
        panel = plan.panel(place, level)
        share = top[lanes(panel, plan.width), :]
        counts = leaf % (plan.sharers * 2**level) == 0
        share = share * jnp.where(counts, 1.0, 0.0)
        own[1, rows] = share - terms[level * plan.width : (level + 1) * plan.width, width:]


def ready_kernel(top_inv, top_coup, inv, coup, inv_t, coup_t):
    for number in range(top_inv.shape[0]):
        inv[number] = top_inv[number]
        inv_t[number] = top_inv[number].T
    for number in range(top_coup.shape[0]):
        coup[number] = top_coup[number]
        coup_t[number] = top_coup[number].T


def turn_kernel(inv_hi, inv_lo, perm_hi, perm_lo, inv_hi_t, inv_lo_t, perm_hi_t, perm_lo_t):
    inv_hi_t[...] = inv_hi[...].T
    inv_lo_t[...] = inv_lo[...].T
    perm_hi_t[...] = perm_hi[...].T
    perm_lo_t[...] = perm_lo[...].T


def climb_kernel(plan, level, value, came, inv, coup, forward, rest):
    _, place, _, _ = plan.here()
    width = plan.width
    above = plan.levels - 1 - level
    result = dot_high(inv[plan.panel(place, level)], value[:width] + came[:width])
    forward[...] = result
    pairs = coup[pl.ds(plan.pair(place, level, level + 1), above)]
    change = dot_high(pairs.reshape(above * width, width), result)
    rest[...] = value[width:] + came[width:] - change


def descend_kernel(plan, *refs):
    levels, width = plan.levels, plan.width
    value, came, inv, inv_t, coup_t = refs[:5]
    forwards = refs[5 : 5 + levels - 1]
    solved, root = refs[5 + levels - 1 :]
    _, place, _, _ = plan.here()
    top = dot_high(inv[0], value[...] + came[...])
    root[...] = top
    found = [None] * levels
    for level in reversed(range(levels)):
        total = top if level == levels - 1 else forwards[level][...]
        for above in reversed(range(level + 1, levels)):
            total = total - dot_high(coup_t[plan.pair(place, level, above)], found[above])
        found[level] = dot_high(inv_t[plan.panel(place, level)], total)
        solved[pl.ds(level * width, width), :] = found[level]


def settle_kernel(plan, count, sides, fresh, *refs):
    refs = list(refs)
    parts = [refs.pop(0) for _ in range(count)]
    lifted, inv_hi_t, inv_lo_t, perm_hi_t, perm_lo_t = refs[:5]
    refs = refs[5:]
    if not fresh:
        refs = refs[1:]
    out, buffer, sems = refs
    _, _, core, half = plan.here()
    width = buffer.shape[2]
    for number, (part, (far, other)) in enumerate(zip(parts, sides)):
        column = 0 if far else width
        group = (1 - half if far else half) * 2 + (1 - core if other else core)
        inner = lifted[:, column : column + width] - dot_split(perm_hi_t[...], perm_lo_t[...], part[...])
        buffer[number] = dot_split(inv_hi_t[...], inv_lo_t[...], inner)
        pltpu.make_async_copy(buffer.at[number], out.at[:, lanes(group, width)], sems.at[number]).start()
    for number, (far, other) in enumerate(sides):
        group = (1 - half if far else half) * 2 + (1 - core if other else core)
        pltpu.make_async_copy(buffer.at[number], out.at[:, lanes(group, width)], sems.at[number]).wait()


def stack_place(step, level, flip):
    if level == step:
        return 2 ** (step + 1) - 2
    half = 2 ** (step - 1 - level)
    if flip < half:
        return stack_place(step - 1, level, flip)
    return 2**step - 1 + stack_place(step - 1, level, flip - half)


def top_kernel(plan, solved, inv_t, coup_t, *refs):
    levels, width = plan.levels, plan.width
    stacks, out = refs[:-1], refs[-1]
    _, place, _, _ = plan.here()
    found = {}
    for level in reversed(range(levels)):
        for flip in range(2 ** (levels - 1 - level)):
            if flip == 0:
                result = solved[pl.ds(level * width, width), :]
            else:
                step = flip.bit_length() - 1 + level
                offset = stack_place(step, level, flip - 2 ** (step - level))
                total = stacks[step][offset]
                for above in reversed(range(level + 1, levels)):
                    total = total - dot_high(
                        coup_t[plan.pair(place, level, above, flip)], found[above, flip >> (above - level)])
                result = dot_high(inv_t[plan.panel(place, level, flip)], total)
            found[level, flip] = result
            out[lanes(plan.panel(place, level, flip), width), :] = result


VMEM_SPEC = pl.BlockSpec(memory_space=pltpu.VMEM)
HBM_SPEC = pl.BlockSpec(memory_space=pltpu.HBM)
ANY_SPEC = pl.BlockSpec(memory_space=pl.ANY)


def call(kernel, outs, args, flops=0, scratch=(), anys=(), alias=None, name=None, after=(), after_hbm=()):
    size = sum(a.size * a.dtype.itemsize for a in args)
    after_hbm = [pltpu.with_memory_space_constraint(a, pltpu.HBM) for a in after_hbm]
    after_specs = [ANY_SPEC] * len(after) + [HBM_SPEC] * len(after_hbm)
    after = list(after) + after_hbm
    count = len(args)

    def body(*refs):
        kernel(*refs[:count], *refs[count + len(after) :])

    specs = [HBM_SPEC if number in anys else VMEM_SPEC for number in range(count)]
    args = [pltpu.with_memory_space_constraint(a, pltpu.HBM if number in anys else pltpu.VMEM)
            for number, a in enumerate(args)]
    return pl.pallas_call(
        body,
        out_shape=[shape for shape, _ in outs],
        in_specs=specs + after_specs,
        out_specs=[spec for _, spec in outs],
        scratch_shapes=list(scratch),
        input_output_aliases=alias or {},
        compiler_params=pltpu.CompilerParams(vmem_limit_bytes=24 * 2**20),
        cost_estimate=pl.CostEstimate(flops=flops, bytes_accessed=size, transcendentals=0),
        name=name,
    )(*args, *after)


def inside(shape, dtype=F32):
    return (pltpu.VMEM(shape, dtype), VMEM_SPEC)


def per_device(rhs_in, rhs_top, leaf_inv, leaf_coupling, coupling_rows, top_inv, top_coupling):
    block_count, order, _ = leaf_inv.shape
    panel_count, width, _ = top_inv.shape
    columns = rhs_top.shape[1]
    path = coupling_rows.shape[1]
    plan = Plan(lax.axis_size("leaf"), lax.axis_size("rhs"), panel_count, width)
    levels = plan.levels
    assert plan.group_count == 4 and block_count == 4 and plan.sharers >= 2

    sent, rhs_own, lifted_other, inv_hi, inv_lo, perm_hi, perm_lo = call(
        functools.partial(lift_kernel, plan, order, columns),
        [inside((2, path, columns)), inside((order, 2 * columns)), inside((order, 2 * columns)),
         inside((order, order), BF16), inside((order, order), BF16),
         inside((path, order), BF16), inside((path, order), BF16)],
        [rhs_in, leaf_inv, leaf_coupling, coupling_rows],
        flops=3 * 2 * 2 * columns * order * (order + path),
        scratch=[pltpu.VMEM((order, 2 * columns), F32), pltpu.VMEM((order, order), F32),
                 pltpu.VMEM((path, order), F32), pltpu.VMEM((1, path), jnp.int32),
                 pltpu.SemaphoreType.DMA((7,))],
        anys=(0, 1, 2, 3), name="lift")
    came = plan.swap_rhs(sent, 1)
    own, lifted_own = call(
        functools.partial(own_kernel, plan, columns),
        [inside((2, path, columns)), inside((order, 2 * columns))],
        [rhs_own, inv_hi, inv_lo, perm_hi, perm_lo, rhs_top],
        flops=3 * 2 * 2 * columns * order * (order + path), name="own")
    far = own[0] + came[0]
    near = own[1] + came[1]
    inv, coup, inv_t, coup_t = call(
        ready_kernel,
        [inside(top_inv.shape), inside(top_coupling.shape), inside(top_inv.shape), inside(top_coupling.shape)],
        [top_inv, top_coupling], flops=10**9, name="ready", after=[far])
    value = near + plan.swap_rhs(far, 2)
    inv_hi_t, inv_lo_t, perm_hi_t, perm_lo_t = call(
        turn_kernel,
        [inside((order, order), BF16), inside((order, order), BF16),
         inside((order, path), BF16), inside((order, path), BF16)],
        [inv_hi, inv_lo, perm_hi, perm_lo], flops=10**9, name="turn", after=[value])
    bit = 1
    while bit < plan.sharers // 2:
        value = value + plan.swap_leaf(value, bit)
        bit *= 2
    came = plan.swap_leaf(value, bit)

    forwards, stacks = [], []
    known = None
    for level in range(levels - 1):
        forward, value = call(
            functools.partial(climb_kernel, plan, level),
            [inside((width, columns)), inside(((levels - 1 - level) * width, columns))],
            [value, came, inv, coup], flops=10**8, name="climb", after=[] if level else [perm_lo_t])
        bit = plan.sharers * 2**level
        came = plan.swap_leaf(value, bit)
        forwards.append(forward)
        known = forward[None] if known is None else jnp.concatenate([known, stacks[-1], forward[None]], 0)
        stacks.append(plan.swap_leaf(known, bit))
    solved, _ = call(
        functools.partial(descend_kernel, plan),
        [inside((path, columns)), inside((width, columns))],
        [value, came, inv, inv_t, coup_t] + forwards, flops=10**8, name="descend")

    far = plan.swap_rhs(solved, 2)
    cross = plan.swap_rhs(solved, 1)
    out_shape = pltpu.HBM((order, plan.group_count * columns), F32)
    work = 3 * 2 * columns * order * (order + path)

    def settle(parts, sides, lifted, out):
        fresh = out is None
        args = list(parts) + [lifted, inv_hi_t, inv_lo_t, perm_hi_t, perm_lo_t] + ([] if fresh else [out])
        count = len(args)
        return call(
            functools.partial(settle_kernel, plan, len(parts), sides, fresh),
            [(out_shape, HBM_SPEC)], args, flops=work * len(parts),
            scratch=[pltpu.VMEM((len(parts), order, columns), F32), pltpu.SemaphoreType.DMA((len(parts),))],
            anys=() if fresh else (count - 1,), alias={} if fresh else {count - 1: 0}, name="settle")[0]

    out = settle([solved], [(False, False)], lifted_own, None)
    out = settle([cross], [(False, True)], lifted_other, out)
    last = plan.swap_rhs(far, 1)
    out = settle([far], [(True, False)], lifted_own, out)
    out = settle([last], [(True, True)], lifted_other, out)
    top = call(
        functools.partial(top_kernel, plan),
        [(jax.ShapeDtypeStruct((panel_count * width, columns), F32), VMEM_SPEC)],
        [solved, inv_t, coup_t] + stacks, flops=10**8, name="top", after_hbm=[out])[0]
    return out, top


def solution(mesh):
    placed = (
        P(("leaf", "rhs"), None),
        P(None, "rhs"),
        P("leaf", None, None),
        P("leaf", None, None),
        P("leaf", None),
        P(),
        P(),
    )
    return jax.shard_map(
        per_device,
        mesh=mesh,
        in_specs=placed,
        out_specs=(P(("leaf", "rhs"), None), P(None, "rhs")),
        check_vma=False,
    )
```

```python
import functools

import jax
import jax.numpy as jnp
from jax import lax
from jax.experimental import pallas as pl
from jax.experimental.pallas import tpu as pltpu
from jax.sharding import PartitionSpec as P

F32, BF16 = jnp.float32, jnp.bfloat16
high = lax.Precision.HIGH


def dot(left, right):
    return jnp.dot(left, right, preferred_element_type=F32)


def dot_high(left, right):
    return jnp.dot(left, right, precision=high, preferred_element_type=F32)


def split(value):
    hi = value.astype(BF16)
    return hi, (value - hi.astype(F32)).astype(BF16)


def dot_split(left_hi, left_lo, right):
    hi, lo = split(right)
    return dot(left_hi, hi) + (dot(left_hi, lo) + dot(left_lo, hi))


def lanes(number, width):
    return pl.ds(pl.multiple_of(number * width, width), width)


class Plan:
    def __init__(self, leaf_count, group_count, panel_count, width):
        self.width = width
        self.levels = (panel_count + 1).bit_length() - 1
        self.bottoms = 2 ** (self.levels - 1)
        self.leaf_count, self.group_count = leaf_count, group_count
        self.sharers = leaf_count // self.bottoms

    def here(self):
        leaf, group = lax.axis_index("leaf"), lax.axis_index("rhs")
        return leaf, leaf // self.sharers, group % 2, group // 2

    def panel(self, place, level, flip=0):
        depth = self.levels - 1 - level
        return 2**depth - 1 + ((place >> level) ^ flip)

    def pair(self, place, below, above, flip=0):
        depth = self.levels - 1 - below
        before = sum(d * 2**d for d in range(depth))
        return before + ((place >> below) ^ flip) * depth + (above - below - 1)

    def swap(self, value, partner):
        pairs = []
        for leaf in range(self.leaf_count):
            for group in range(self.group_count):
                to_leaf, to_group = partner(leaf, group)
                pairs.append((leaf * self.group_count + group, to_leaf * self.group_count + to_group))
        return lax.ppermute(value, ("leaf", "rhs"), pairs)

    def swap_rhs(self, value, bit):
        return self.swap(value, lambda leaf, group: (leaf, group ^ bit))

    def swap_leaf(self, value, bit):
        return self.swap(value, lambda leaf, group: (leaf ^ bit, group))


def lift_kernel(plan, order, width, rhs, inv, coupling, rows, sent, rhs_own, lifted, inv_hi, inv_lo,
                perm_hi, perm_lo, rhs_buf, inv_buf, coup_buf, row_buf, sems):
    _, _, core, half = plan.here()
    block = half * 2 + core
    path = coupling.shape[1]
    copies = [
        pltpu.make_async_copy(rows.at[pl.ds(block, 1)], row_buf, sems.at[0]),
        pltpu.make_async_copy(coupling.at[block], coup_buf, sems.at[1]),
    ]
    for number, side in enumerate((1 - half, half)):
        copies.append(pltpu.make_async_copy(
            rhs.at[:, lanes(side * 2 + 1 - core, width)],
            rhs_buf.at[:, pl.ds(number * width, width)], sems.at[2 + number]))
    copies.append(pltpu.make_async_copy(inv.at[block], inv_buf, sems.at[4]))
    for number, side in enumerate((1 - half, half)):
        copies.append(pltpu.make_async_copy(
            rhs.at[:, lanes(side * 2 + core, width)],
            rhs_own.at[:, pl.ds(number * width, width)], sems.at[5 + number]))
    for copy in copies:
        copy.start()
    copies[0].wait()
    chosen = (lax.broadcasted_iota(jnp.int32, (path, path), 0) == row_buf[...]).astype(BF16)
    copies[1].wait()
    coup_hi, coup_lo = split(coup_buf[...])
    perm_hi[...] = dot(chosen, coup_hi).astype(BF16)
    perm_lo[...] = dot(chosen, coup_lo).astype(BF16)
    copies[2].wait()
    copies[3].wait()
    copies[4].wait()
    hi, lo = split(inv_buf[...])
    inv_hi[...] = hi
    inv_lo[...] = lo
    result = dot_split(hi, lo, rhs_buf[...])
    lifted[...] = result
    terms = dot_split(perm_hi[...], perm_lo[...], result)
    sent[0] = -terms[:, :width]
    sent[1] = -terms[:, width:]
    copies[5].wait()
    copies[6].wait()


def own_kernel(plan, width, rhs_own, inv_hi, inv_lo, perm_hi, perm_lo, top, own, lifted):
    leaf, place, _, _ = plan.here()
    result = dot_split(inv_hi[...], inv_lo[...], rhs_own[...])
    lifted[...] = result
    terms = dot_split(perm_hi[...], perm_lo[...], result)
    own[0] = -terms[:, :width]
    for level in range(plan.levels):
        rows = pl.ds(level * plan.width, plan.width)
        panel = plan.panel(place, level)
        share = top[lanes(panel, plan.width), :]
        counts = leaf % (plan.sharers * 2**level) == 0
        share = share * jnp.where(counts, 1.0, 0.0)
        own[1, rows] = share - terms[level * plan.width : (level + 1) * plan.width, width:]


def ready_kernel(levels, top_inv, top_coup, inv, coup, back_hi, back_lo):
    width = top_inv.shape[1]
    first = 0
    for number in range(top_inv.shape[0]):
        depth = (number + 1).bit_length() - 1
        inv[number] = top_inv[number]
        turned = top_inv[number].T
        back_hi[number, :, :width], back_lo[number, :, :width] = split(turned)
        for step in range(depth):
            pair = first + step
            coup[pair] = top_coup[pair]
            columns = pl.ds((step + 1) * width, width)
            back_hi[number, :, columns], back_lo[number, :, columns] = split(
                -dot_high(turned, top_coup[pair].T))
        first += depth


def turn_kernel(inv_hi, inv_lo, perm_hi, perm_lo, lifted_own, lifted_other, base_own, base_other, gain_hi, gain_lo, token):
    hi, lo = inv_hi[...].T, inv_lo[...].T
    turned_hi, turned_lo = perm_hi[...].T, perm_lo[...].T
    gain = dot(hi, turned_hi) + (dot(hi, turned_lo) + dot(lo, turned_hi))
    gain_hi[...], gain_lo[...] = split(gain)
    base_own[...] = dot_split(hi, lo, lifted_own[...])
    base_other[...] = dot_split(hi, lo, lifted_other[...])
    token[...] = jnp.zeros_like(token)


def climb_kernel(plan, level, value, came, inv, coup, forward, rest):
    _, place, _, _ = plan.here()
    width = plan.width
    above = plan.levels - 1 - level
    result = dot_high(inv[plan.panel(place, level)], value[:width] + came[:width])
    forward[...] = result
    pairs = coup[pl.ds(plan.pair(place, level, level + 1), above)]
    change = dot_high(pairs.reshape(above * width, width), result)
    rest[...] = value[width:] + came[width:] - change


def backward(plan, back_hi, back_lo, panel, level, forward, above):
    depth = plan.width * (plan.levels - level)
    known = jnp.concatenate([forward] + above, 0) if above else forward
    return dot_split(back_hi[panel, :, :depth], back_lo[panel, :, :depth], known)


def descend_kernel(plan, *refs):
    levels, width = plan.levels, plan.width
    value, came, inv, back_hi, back_lo = refs[:5]
    forwards = refs[5 : 5 + levels - 1]
    solved = refs[5 + levels - 1]
    _, place, _, _ = plan.here()
    top = dot_high(inv[0], value[...] + came[...])
    above = []
    for level in reversed(range(levels)):
        forward = top if level == levels - 1 else forwards[level][...]
        result = backward(plan, back_hi, back_lo, plan.panel(place, level), level, forward, above)
        solved[pl.ds(level * width, width), :] = result
        above = [result] + above


def settled(base, gain_hi, gain_lo, part, column, width):
    change = dot_split(gain_hi[...], gain_lo[...], part[...])
    return base[:, column : column + width] - change


def settle_kernel(width, column, part, base, gain_hi, gain_lo, out, token):
    out[...] = settled(base, gain_hi, gain_lo, part, column, width)
    token[...] = jnp.zeros_like(token)


def last_kernel(plan, width, part, base, gain_hi, gain_lo, own, far, out, buffer, sems):
    _, _, core, half = plan.here()
    groups = ((1 - half) * 2 + core, half * 2 + core, (1 - half) * 2 + 1 - core, half * 2 + 1 - core)
    copies = [pltpu.make_async_copy(done, out.at[:, lanes(group, width)], sems.at[number])
              for number, (done, group) in enumerate(zip((
                  far, own, buffer.at[:, :width], buffer.at[:, width:]), groups))]
    copies[0].start()
    copies[1].start()
    known = jnp.concatenate([part[0], part[1]], 1)
    buffer[...] = base[...] - dot_split(gain_hi[...], gain_lo[...], known)
    copies[2].start()
    copies[3].start()
    for copy in copies:
        copy.wait()


def stack_place(step, level, flip):
    if level == step:
        return 2 ** (step + 1) - 2
    half = 2 ** (step - 1 - level)
    if flip < half:
        return stack_place(step - 1, level, flip)
    return 2**step - 1 + stack_place(step - 1, level, flip - half)


def top_kernel(plan, solved, back_hi, back_lo, *refs):
    levels, width = plan.levels, plan.width
    stacks, out = refs[:-1], refs[-1]
    _, place, _, _ = plan.here()
    found = {}
    for level in reversed(range(levels)):
        for flip in range(2 ** (levels - 1 - level)):
            panel = plan.panel(place, level, flip)
            if flip == 0:
                result = solved[pl.ds(level * width, width), :]
            else:
                step = flip.bit_length() - 1 + level
                forward = stacks[step][stack_place(step, level, flip - 2 ** (step - level))]
                above = [found[up, flip >> (up - level)] for up in range(level + 1, levels)]
                result = backward(plan, back_hi, back_lo, panel, level, forward, above)
            found[level, flip] = result
            out[lanes(panel, width), :] = result


VMEM_SPEC = pl.BlockSpec(memory_space=pltpu.VMEM)
HBM_SPEC = pl.BlockSpec(memory_space=pltpu.HBM)
ANY_SPEC = pl.BlockSpec(memory_space=pl.ANY)


def call(kernel, outs, args, scratch=(), anys=(), name=None, after=(), after_hbm=(), flops=1000):
    after_hbm = [pltpu.with_memory_space_constraint(a, pltpu.HBM) for a in after_hbm]
    after_specs = [ANY_SPEC] * len(after) + [HBM_SPEC] * len(after_hbm)
    after = list(after) + after_hbm
    count = len(args)

    def body(*refs):
        kernel(*refs[:count], *refs[count + len(after) :])

    specs = [HBM_SPEC if number in anys else VMEM_SPEC for number in range(count)]
    args = [pltpu.with_memory_space_constraint(a, pltpu.HBM if number in anys else pltpu.VMEM)
            for number, a in enumerate(args)]
    return pl.pallas_call(
        body,
        out_shape=[shape for shape, _ in outs],
        in_specs=specs + after_specs,
        out_specs=[spec for _, spec in outs],
        scratch_shapes=list(scratch),
        compiler_params=pltpu.CompilerParams(vmem_limit_bytes=24 * 2**20),
        cost_estimate=pl.CostEstimate(flops=flops, bytes_accessed=1000, transcendentals=0),
        name=name,
    )(*args, *after)


def inside(shape, dtype=F32):
    return (pltpu.VMEM(shape, dtype), VMEM_SPEC)


def per_device(rhs_in, rhs_top, leaf_inv, leaf_coupling, coupling_rows, top_inv, top_coupling):
    block_count, order, _ = leaf_inv.shape
    panel_count, width, _ = top_inv.shape
    columns = rhs_top.shape[1]
    path = coupling_rows.shape[1]
    plan = Plan(lax.axis_size("leaf"), lax.axis_size("rhs"), panel_count, width)
    levels = plan.levels
    assert plan.group_count == 4 and block_count == 4 and plan.sharers >= 2

    sent, rhs_own, lifted_other, inv_hi, inv_lo, perm_hi, perm_lo = call(
        functools.partial(lift_kernel, plan, order, columns),
        [inside((2, path, columns)), inside((order, 2 * columns)), inside((order, 2 * columns)),
         inside((order, order), BF16), inside((order, order), BF16),
         inside((path, order), BF16), inside((path, order), BF16)],
        [rhs_in, leaf_inv, leaf_coupling, coupling_rows],
        scratch=[pltpu.VMEM((order, 2 * columns), F32), pltpu.VMEM((order, order), F32),
                 pltpu.VMEM((path, order), F32), pltpu.VMEM((1, path), jnp.int32),
                 pltpu.SemaphoreType.DMA((7,))],
        anys=(0, 1, 2, 3), name="lift")
    came = plan.swap_rhs(sent, 1)
    own, lifted_own = call(
        functools.partial(own_kernel, plan, columns),
        [inside((2, path, columns)), inside((order, 2 * columns))],
        [rhs_own, inv_hi, inv_lo, perm_hi, perm_lo, rhs_top], name="own")
    far = own[0] + came[0]
    near = own[1] + came[1]
    base_own, base_other, gain_hi, gain_lo, token = call(
        turn_kernel,
        [inside((order, 2 * columns)), inside((order, 2 * columns)),
         inside((order, path), BF16), inside((order, path), BF16), inside((8, columns))],
        [inv_hi, inv_lo, perm_hi, perm_lo, lifted_own, lifted_other], name="turn", after=[far])
    value = near + plan.swap_rhs(far, 2) + token[:1]
    backs = (panel_count, width, levels * width)
    inv, coup, back_hi, back_lo = call(
        functools.partial(ready_kernel, levels),
        [inside(top_inv.shape), inside(top_coupling.shape), inside(backs, BF16), inside(backs, BF16)],
        [top_inv, top_coupling], name="ready", after=[value])
    bit = 1
    while bit < plan.sharers // 2:
        value = value + plan.swap_leaf(value, bit)
        bit *= 2
    came = plan.swap_leaf(value, bit)

    forwards, stacks, known = [], [], []
    for level in range(levels - 1):
        forward, value = call(
            functools.partial(climb_kernel, plan, level),
            [inside((width, columns)), inside(((levels - 1 - level) * width, columns))],
            [value, came, inv, coup], name="climb")
        bit = plan.sharers * 2**level
        came = plan.swap_leaf(value, bit)
        forwards.append(forward)
        known = known + stacks[-1:] + [forward[None]]
        stacks.append(plan.swap_leaf(jnp.concatenate(known, 0), bit))
    solved = call(
        functools.partial(descend_kernel, plan),
        [inside((path, columns))],
        [value, came, inv, back_hi, back_lo] + forwards, name="descend", after=stacks[:-1])[0]

    far = plan.swap_rhs(solved, 2)

    def settle(part, base, column):
        return call(
            functools.partial(settle_kernel, columns, column),
            [inside((order, columns)), inside((8, columns))],
            [part, base, gain_hi, gain_lo], name="settle")

    own, token = settle(solved, base_own, columns)
    pair = jnp.stack([far + token[:1], solved])
    last = plan.swap_rhs(pair, 1)
    far, token = settle(far, base_own, 0)
    top = call(
        functools.partial(top_kernel, plan),
        [(jax.ShapeDtypeStruct((panel_count * width, columns), F32), VMEM_SPEC)],
        [solved, back_hi, back_lo] + stacks, name="top", after=[token], flops=5 * 10**9)[0]
    out = call(
        functools.partial(last_kernel, plan, columns),
        [(pltpu.HBM((order, plan.group_count * columns), F32), HBM_SPEC)],
        [last, base_other, gain_hi, gain_lo, own, far],
        scratch=[pltpu.VMEM((order, 2 * columns), F32), pltpu.SemaphoreType.DMA((4,))], name="last",
        after_hbm=[top])[0]
    return out, top


def solution(mesh):
    placed = (
        P(("leaf", "rhs"), None),
        P(None, "rhs"),
        P("leaf", None, None),
        P("leaf", None, None),
        P("leaf", None),
        P(),
        P(),
    )
    return jax.shard_map(
        per_device,
        mesh=mesh,
        in_specs=placed,
        out_specs=(P(("leaf", "rhs"), None), P(None, "rhs")),
        check_vma=False,
    )
```

```python
import functools

import jax
import jax.numpy as jnp
from jax import lax
from jax.experimental import pallas as pl
from jax.experimental.pallas import tpu as pltpu
from jax.sharding import PartitionSpec as P

F32, BF16 = jnp.float32, jnp.bfloat16
high = lax.Precision.HIGH


def dot(left, right):
    return jnp.dot(left, right, preferred_element_type=F32)


def dot_high(left, right):
    return jnp.dot(left, right, precision=high, preferred_element_type=F32)


def split(value):
    hi = value.astype(BF16)
    return hi, (value - hi.astype(F32)).astype(BF16)


def dot_split(left_hi, left_lo, right):
    hi, lo = split(right)
    return dot(left_hi, hi) + (dot(left_hi, lo) + dot(left_lo, hi))


def lanes(number, width):
    return pl.ds(pl.multiple_of(number * width, width), width)


class Plan:
    def __init__(self, leaf_count, group_count, panel_count, width):
        self.width = width
        self.levels = (panel_count + 1).bit_length() - 1
        self.bottoms = 2 ** (self.levels - 1)
        self.leaf_count, self.group_count = leaf_count, group_count
        self.sharers = leaf_count // self.bottoms

    def here(self):
        leaf, group = lax.axis_index("leaf"), lax.axis_index("rhs")
        return leaf, leaf // self.sharers, group % 2, group // 2

    def panel(self, place, level, flip=0):
        depth = self.levels - 1 - level
        return 2**depth - 1 + ((place >> level) ^ flip)

    def pair(self, place, below, above, flip=0):
        depth = self.levels - 1 - below
        before = sum(d * 2**d for d in range(depth))
        return before + ((place >> below) ^ flip) * depth + (above - below - 1)

    def swap(self, value, partner):
        pairs = []
        for leaf in range(self.leaf_count):
            for group in range(self.group_count):
                to_leaf, to_group = partner(leaf, group)
                pairs.append((leaf * self.group_count + group, to_leaf * self.group_count + to_group))
        return lax.ppermute(value, ("leaf", "rhs"), pairs)

    def swap_rhs(self, value, bit):
        return self.swap(value, lambda leaf, group: (leaf, group ^ bit))

    def swap_leaf(self, value, bit):
        return self.swap(value, lambda leaf, group: (leaf ^ bit, group))


def lift_and_couple(rhs_hi, rhs_lo, inv_hi, inv_lo, perm_hi, perm_lo, lifted, sent, hi_buf, lo_buf, step):
    width = sent.shape[2]
    for start in range(0, lifted.shape[0], step):
        rows = slice(start, start + step)
        part = dot(inv_hi[rows], rhs_hi) + (dot(inv_hi[rows], rhs_lo) + dot(inv_lo[rows], rhs_hi))
        lifted[rows] = part
        hi_buf[rows], lo_buf[rows] = split(part)
    step = sent.shape[1] // 2
    for start in range(0, sent.shape[1], step):
        rows = slice(start, start + step)
        part = dot(perm_hi[rows], hi_buf[...]) + (
            dot(perm_hi[rows], lo_buf[...]) + dot(perm_lo[rows], hi_buf[...]))
        sent[0, rows] = -part[:, :width]
        sent[1, rows] = -part[:, width:]


def lift_kernel(plan, order, width, rhs, inv, coupling, rows, sent, rhs_own, lifted, inv_hi, inv_lo,
                perm_hi, perm_lo, rhs_buf, inv_buf, coup_buf, row_buf, hi_buf, lo_buf, sems):
    _, _, core, half = plan.here()
    block = half * 2 + core
    path = coupling.shape[1]
    copies = [
        pltpu.make_async_copy(rows.at[pl.ds(block, 1)], row_buf, sems.at[0]),
        pltpu.make_async_copy(coupling.at[block], coup_buf, sems.at[1]),
    ]
    for number, side in enumerate((1 - half, half)):
        copies.append(pltpu.make_async_copy(
            rhs.at[:, lanes(side * 2 + 1 - core, width)],
            rhs_buf.at[:, pl.ds(number * width, width)], sems.at[2 + number]))
    copies.append(pltpu.make_async_copy(inv.at[block], inv_buf, sems.at[4]))
    for number, side in enumerate((1 - half, half)):
        copies.append(pltpu.make_async_copy(
            rhs.at[:, lanes(side * 2 + core, width)],
            rhs_own.at[:, pl.ds(number * width, width)], sems.at[5 + number]))
    for copy in copies:
        copy.start()
    copies[0].wait()
    chosen = (lax.broadcasted_iota(jnp.int32, (path, path), 0) == row_buf[...]).astype(BF16)
    copies[1].wait()
    coup_hi, coup_lo = split(coup_buf[...])
    perm_hi[...] = dot(chosen, coup_hi).astype(BF16)
    perm_lo[...] = dot(chosen, coup_lo).astype(BF16)
    copies[2].wait()
    copies[3].wait()
    rhs_hi, rhs_lo = split(rhs_buf[...])
    copies[4].wait()
    inv_hi[...], inv_lo[...] = split(inv_buf[...])
    lift_and_couple(rhs_hi, rhs_lo, inv_hi, inv_lo, perm_hi, perm_lo, lifted, sent, hi_buf, lo_buf, order // 4)
    copies[5].wait()
    copies[6].wait()


def own_kernel(plan, rhs_own, inv_hi, inv_lo, perm_hi, perm_lo, top, own, lifted, hi_buf, lo_buf):
    leaf, place, _, _ = plan.here()
    rhs_hi, rhs_lo = split(rhs_own[...])
    lift_and_couple(rhs_hi, rhs_lo, inv_hi, inv_lo, perm_hi, perm_lo, lifted, own, hi_buf, lo_buf, lifted.shape[0] // 2)
    for level in range(plan.levels):
        @pl.when(leaf % (plan.sharers * 2**level) == 0)
        def _():
            own[1, level * plan.width : (level + 1) * plan.width] += top[lanes(plan.panel(place, level), plan.width), :]


def ready_kernel(levels, top_inv, top_coup, inv, coup, back_hi, back_lo):
    width = top_inv.shape[1]
    first = 0
    for number in range(top_inv.shape[0]):
        depth = (number + 1).bit_length() - 1
        inv[number] = top_inv[number]
        turned = top_inv[number].T
        back_hi[number, :, :width], back_lo[number, :, :width] = split(turned)
        for step in range(depth):
            pair = first + step
            coup[pair] = top_coup[pair]
            columns = pl.ds((step + 1) * width, width)
            back_hi[number, :, columns], back_lo[number, :, columns] = split(
                -dot_high(turned, top_coup[pair].T))
        first += depth


def turn_kernel(inv_hi, inv_lo, perm_hi, perm_lo, lifted_own, lifted_other, base_own, base_other, gain_hi, gain_lo, token):
    hi, lo = inv_hi[...].T, inv_lo[...].T
    turned_hi, turned_lo = perm_hi[...].T, perm_lo[...].T
    gain = dot(hi, turned_hi) + (dot(hi, turned_lo) + dot(lo, turned_hi))
    gain_hi[...], gain_lo[...] = split(gain)
    base_own[...] = dot_split(hi, lo, lifted_own[...])
    base_other[...] = dot_split(hi, lo, lifted_other[...])
    token[...] = jnp.zeros_like(token)


def climb_kernel(plan, level, value, came, inv, coup, forward, rest):
    _, place, _, _ = plan.here()
    width = plan.width
    above = plan.levels - 1 - level
    result = dot_high(inv[plan.panel(place, level)], value[:width] + came[:width])
    forward[...] = result
    pairs = coup[pl.ds(plan.pair(place, level, level + 1), above)]
    change = dot_high(pairs.reshape(above * width, width), result)
    rest[...] = value[width:] + came[width:] - change


def backward(plan, back_hi, back_lo, panel, level, forward, above):
    depth = plan.width * (plan.levels - level)
    known = jnp.concatenate([forward] + above, 0) if above else forward
    return dot_split(back_hi[panel, :, :depth], back_lo[panel, :, :depth], known)


def halve_kernel(plan, *refs):
    leaf, _, _, _ = plan.here()
    out, number = refs[-1], 0
    for ref in refs[:-1]:
        for panel in range(ref.shape[0]):
            out[number] = ref[panel, lanes(leaf % 2, plan.width // 2), :]
            number += 1


def descend_kernel(plan, *refs):
    levels, width = plan.levels, plan.width
    value, came, inv, back_hi, back_lo = refs[:5]
    forwards = refs[5 : 5 + levels - 1]
    solved = refs[5 + levels - 1]
    _, place, _, _ = plan.here()
    top = dot_high(inv[0], value[...] + came[...])
    above = []
    for level in reversed(range(levels)):
        forward = top if level == levels - 1 else forwards[level][...]
        result = backward(plan, back_hi, back_lo, plan.panel(place, level), level, forward, above)
        solved[pl.ds(level * width, width), :] = result
        above = [result] + above


def settled(base, gain_hi, gain_lo, part, column, width):
    change = dot_split(gain_hi[...], gain_lo[...], part[...])
    return base[:, column : column + width] - change


def settle_kernel(width, column, part, base, gain_hi, gain_lo, out, token):
    out[...] = settled(base, gain_hi, gain_lo, part, column, width)
    token[...] = jnp.zeros_like(token)


def last_kernel(plan, width, part, base, gain_hi, gain_lo, own, far, out, buffer, sems):
    _, _, core, half = plan.here()
    groups = ((1 - half) * 2 + core, half * 2 + core, (1 - half) * 2 + 1 - core, half * 2 + 1 - core)
    copies = [pltpu.make_async_copy(done, out.at[:, lanes(group, width)], sems.at[number])
              for number, (done, group) in enumerate(zip((
                  far, own, buffer.at[:, :width], buffer.at[:, width:]), groups))]
    copies[0].start()
    copies[1].start()
    known = jnp.concatenate([part[0], part[1]], 1)
    buffer[...] = base[...] - dot_split(gain_hi[...], gain_lo[...], known)
    copies[2].start()
    copies[3].start()
    for copy in copies:
        copy.wait()


def stack_place(step, level, flip):
    if level == step:
        return 2 ** (step + 1) - 2
    half = 2 ** (step - 1 - level)
    if flip < half:
        return stack_place(step - 1, level, flip)
    return 2**step - 1 + stack_place(step - 1, level, flip - half)


def top_kernel(plan, solved, back_hi, back_lo, *refs):
    levels, width = plan.levels, plan.width
    stacks, out = refs[:-1], refs[-1]
    leaf, place, _, _ = plan.here()
    second = leaf % 2 == 1
    found = {}
    for level in reversed(range(levels)):
        for flip in range(2 ** (levels - 1 - level)):
            panel = plan.panel(place, level, flip)
            if flip == 0:
                result = solved[pl.ds(level * width, width), :]
            else:
                step = flip.bit_length() - 1 + level
                number = stack_place(step, level, flip - 2 ** (step - level))
                forward = stacks[step][number]
                if step == levels - 2:
                    other = stacks[step + 1][number]
                    forward = jnp.concatenate(
                        [jnp.where(second, other, forward), jnp.where(second, forward, other)], 0)
                above = [found[up, flip >> (up - level)] for up in range(level + 1, levels)]
                result = backward(plan, back_hi, back_lo, panel, level, forward, above)
            found[level, flip] = result
            out[lanes(panel, width), :] = result


VMEM_SPEC = pl.BlockSpec(memory_space=pltpu.VMEM)
HBM_SPEC = pl.BlockSpec(memory_space=pltpu.HBM)
ANY_SPEC = pl.BlockSpec(memory_space=pl.ANY)


def call(kernel, outs, args, scratch=(), anys=(), name=None, after=(), after_hbm=(), flops=1000):
    after_hbm = [pltpu.with_memory_space_constraint(a, pltpu.HBM) for a in after_hbm]
    after_specs = [ANY_SPEC] * len(after) + [HBM_SPEC] * len(after_hbm)
    after = list(after) + after_hbm
    count = len(args)

    def body(*refs):
        kernel(*refs[:count], *refs[count + len(after) :])

    specs = [HBM_SPEC if number in anys else VMEM_SPEC for number in range(count)]
    args = [pltpu.with_memory_space_constraint(a, pltpu.HBM if number in anys else pltpu.VMEM)
            for number, a in enumerate(args)]
    return pl.pallas_call(
        body,
        out_shape=[shape for shape, _ in outs],
        in_specs=specs + after_specs,
        out_specs=[spec for _, spec in outs],
        scratch_shapes=list(scratch),
        compiler_params=pltpu.CompilerParams(vmem_limit_bytes=12 * 2**20),
        cost_estimate=pl.CostEstimate(flops=flops, bytes_accessed=1000, transcendentals=0),
        name=name,
    )(*args, *after)


def inside(shape, dtype=F32):
    return (pltpu.VMEM(shape, dtype), VMEM_SPEC)


def per_device(rhs_in, rhs_top, leaf_inv, leaf_coupling, coupling_rows, top_inv, top_coupling):
    block_count, order, _ = leaf_inv.shape
    panel_count, width, _ = top_inv.shape
    columns = rhs_top.shape[1]
    path = coupling_rows.shape[1]
    plan = Plan(lax.axis_size("leaf"), lax.axis_size("rhs"), panel_count, width)
    levels = plan.levels
    assert plan.group_count == 4 and block_count == 4 and plan.sharers >= 2

    halves = [pltpu.VMEM((order, 2 * columns), BF16)] * 2
    sent, rhs_own, lifted_other, inv_hi, inv_lo, perm_hi, perm_lo = call(
        functools.partial(lift_kernel, plan, order, columns),
        [inside((2, path, columns)), inside((order, 2 * columns)), inside((order, 2 * columns)),
         inside((order, order), BF16), inside((order, order), BF16),
         inside((path, order), BF16), inside((path, order), BF16)],
        [rhs_in, leaf_inv, leaf_coupling, coupling_rows],
        scratch=[pltpu.VMEM((order, 2 * columns), F32), pltpu.VMEM((order, order), F32),
                 pltpu.VMEM((path, order), F32), pltpu.VMEM((1, path), jnp.int32), *halves,
                 pltpu.SemaphoreType.DMA((7,))],
        anys=(0, 1, 2, 3), name="lift")
    came = plan.swap_rhs(sent, 1)
    own, lifted_own = call(
        functools.partial(own_kernel, plan),
        [inside((2, path, columns)), inside((order, 2 * columns))],
        [rhs_own, inv_hi, inv_lo, perm_hi, perm_lo, rhs_top], scratch=halves, name="own")
    far = own[0] + came[0]
    near = own[1] + came[1]
    base_own, base_other, gain_hi, gain_lo, token = call(
        turn_kernel,
        [inside((order, 2 * columns)), inside((order, 2 * columns)),
         inside((order, path), BF16), inside((order, path), BF16), inside((8, columns))],
        [inv_hi, inv_lo, perm_hi, perm_lo, lifted_own, lifted_other], name="turn", after=[far])
    value = near + plan.swap_rhs(far, 2) + token[:1]
    backs = (panel_count, width, levels * width)
    inv, coup, back_hi, back_lo = call(
        functools.partial(ready_kernel, levels),
        [inside(top_inv.shape), inside(top_coupling.shape), inside(backs, BF16), inside(backs, BF16)],
        [top_inv, top_coupling], name="ready", after=[value])
    bit = 1
    while bit < plan.sharers // 2:
        value = value + plan.swap_leaf(value, bit)
        bit *= 2
    came = plan.swap_leaf(value, bit)

    forwards, stacks, known = [], [], []
    for level in range(levels - 1):
        forward, value = call(
            functools.partial(climb_kernel, plan, level),
            [inside((width, columns)), inside(((levels - 1 - level) * width, columns))],
            [value, came, inv, coup], name="climb")
        bit = plan.sharers * 2**level
        came = plan.swap_leaf(value, bit)
        forwards.append(forward)
        known = known + stacks[-1:] + [forward[None]]
        if level == levels - 2:
            stack = call(
                functools.partial(halve_kernel, plan),
                [inside((2 ** (level + 1) - 1, width // 2, columns))], known, name="halve", after=[value])[0]
        else:
            stack = jnp.concatenate(known, 0)
        stacks.append(plan.swap_leaf(stack, bit))
    solved = call(
        functools.partial(descend_kernel, plan),
        [inside((path, columns))],
        [value, came, inv, back_hi, back_lo] + forwards, name="descend", after=stacks[:-1])[0]

    far = plan.swap_rhs(solved, 2)

    def settle(part, base, column):
        return call(
            functools.partial(settle_kernel, columns, column),
            [inside((order, columns)), inside((8, columns))],
            [part, base, gain_hi, gain_lo], name="settle")

    own, token = settle(solved, base_own, columns)
    stacks.append(plan.swap_leaf(stacks[-1] + token[:1], 1))
    pair = jnp.stack([far + token[:1], solved])
    last = plan.swap_rhs(pair, 1)
    far, token = settle(far, base_own, 0)
    top = call(
        functools.partial(top_kernel, plan),
        [(jax.ShapeDtypeStruct((panel_count * width, columns), F32), VMEM_SPEC)],
        [solved, back_hi, back_lo] + stacks, name="top", after=[token], flops=5 * 10**9)[0]
    out = call(
        functools.partial(last_kernel, plan, columns),
        [(pltpu.HBM((order, plan.group_count * columns), F32), HBM_SPEC)],
        [last, base_other, gain_hi, gain_lo, own, far],
        scratch=[pltpu.VMEM((order, 2 * columns), F32), pltpu.SemaphoreType.DMA((4,))], name="last",
        after_hbm=[top])[0]
    return out, top


def solution(mesh):
    placed = (
        P(("leaf", "rhs"), None),
        P(None, "rhs"),
        P("leaf", None, None),
        P("leaf", None, None),
        P("leaf", None),
        P(),
        P(),
    )
    return jax.shard_map(
        per_device,
        mesh=mesh,
        in_specs=placed,
        out_specs=(P(("leaf", "rhs"), None), P(None, "rhs")),
        check_vma=False,
    )
```

```python
import functools

import jax
import jax.numpy as jnp
from jax import lax
from jax.experimental import pallas as pl
from jax.experimental.pallas import tpu as pltpu
from jax.sharding import PartitionSpec as P

F32, BF16 = jnp.float32, jnp.bfloat16
high = lax.Precision.HIGH


def dot(left, right):
    return jnp.dot(left, right, preferred_element_type=F32)


def dot_high(left, right):
    return jnp.dot(left, right, precision=high, preferred_element_type=F32)


def split(value):
    hi = value.astype(BF16)
    return hi, (value - hi.astype(F32)).astype(BF16)


def dot_split(left_hi, left_lo, right):
    hi, lo = split(right)
    return dot(left_hi, hi) + (dot(left_hi, lo) + dot(left_lo, hi))


def lanes(number, width):
    return pl.ds(pl.multiple_of(number * width, width), width)


class Plan:
    def __init__(self, leaf_count, group_count, panel_count, width):
        self.width = width
        self.levels = (panel_count + 1).bit_length() - 1
        self.bottoms = 2 ** (self.levels - 1)
        self.leaf_count, self.group_count = leaf_count, group_count
        self.sharers = leaf_count // self.bottoms

    def here(self):
        leaf, group = lax.axis_index("leaf"), lax.axis_index("rhs")
        return leaf, leaf // self.sharers, group % 2, group // 2

    def panel(self, place, level, flip=0):
        depth = self.levels - 1 - level
        return 2**depth - 1 + ((place >> level) ^ flip)

    def pair(self, place, below, above, flip=0):
        depth = self.levels - 1 - below
        before = sum(d * 2**d for d in range(depth))
        return before + ((place >> below) ^ flip) * depth + (above - below - 1)

    def swap(self, value, partner):
        pairs = []
        for leaf in range(self.leaf_count):
            for group in range(self.group_count):
                to_leaf, to_group = partner(leaf, group)
                pairs.append((leaf * self.group_count + group, to_leaf * self.group_count + to_group))
        return lax.ppermute(value, ("leaf", "rhs"), pairs)

    def swap_rhs(self, value, bit):
        return self.swap(value, lambda leaf, group: (leaf, group ^ bit))

    def swap_leaf(self, value, bit):
        return self.swap(value, lambda leaf, group: (leaf ^ bit, group))


def lift_and_couple(rhs_hi, rhs_lo, inv_hi, inv_lo, perm_hi, perm_lo, lifted, first, second, hi_buf, lo_buf, step):
    path, width = perm_hi.shape[0], first.shape[1]
    cut = first.shape[0]
    for start in range(0, lifted.shape[0], step):
        rows = slice(start, start + step)
        part = dot(inv_hi[rows], rhs_hi) + (dot(inv_hi[rows], rhs_lo) + dot(inv_lo[rows], rhs_hi))
        lifted[rows] = part
        hi_buf[rows], lo_buf[rows] = split(part)
    step = path // 2
    for start in range(0, path, step):
        rows = slice(start, start + step)
        part = dot(perm_hi[rows], hi_buf[...]) + (
            dot(perm_hi[rows], lo_buf[...]) + dot(perm_lo[rows], hi_buf[...]))
        if start < cut:
            first[start : min(start + step, cut)] = -part[: min(step, cut - start), :width]
        if start + step > cut:
            skip = max(cut - start, 0)
            second[start + skip - cut : start + step - cut] = -part[skip:, :width]
        second[path - cut + start : path - cut + start + step] = -part[:, width:]


def lift_kernel(plan, order, width, rhs, inv, coupling, rows, first, second, rhs_own, lifted, inv_hi, inv_lo,
                perm_hi, perm_lo, rhs_buf, inv_buf, coup_buf, row_buf, hi_buf, lo_buf, sems):
    _, _, core, half = plan.here()
    block = half * 2 + core
    path = coupling.shape[1]
    copies = [
        pltpu.make_async_copy(rows.at[pl.ds(block, 1)], row_buf, sems.at[0]),
        pltpu.make_async_copy(coupling.at[block], coup_buf, sems.at[1]),
    ]
    for number, side in enumerate((1 - half, half)):
        copies.append(pltpu.make_async_copy(
            rhs.at[:, lanes(side * 2 + 1 - core, width)],
            rhs_buf.at[:, pl.ds(number * width, width)], sems.at[2 + number]))
    copies.append(pltpu.make_async_copy(inv.at[block], inv_buf, sems.at[4]))
    for number, side in enumerate((1 - half, half)):
        copies.append(pltpu.make_async_copy(
            rhs.at[:, lanes(side * 2 + core, width)],
            rhs_own.at[:, pl.ds(number * width, width)], sems.at[5 + number]))
    for copy in copies:
        copy.start()
    copies[0].wait()
    chosen = (lax.broadcasted_iota(jnp.int32, (path, path), 0) == row_buf[...]).astype(BF16)
    copies[1].wait()
    coup_hi, coup_lo = split(coup_buf[...])
    perm_hi[...] = dot(chosen, coup_hi).astype(BF16)
    perm_lo[...] = dot(chosen, coup_lo).astype(BF16)
    copies[2].wait()
    copies[3].wait()
    rhs_hi, rhs_lo = split(rhs_buf[...])
    copies[4].wait()
    inv_hi[...], inv_lo[...] = split(inv_buf[...])
    lift_and_couple(rhs_hi, rhs_lo, inv_hi, inv_lo, perm_hi, perm_lo, lifted, first, second, hi_buf, lo_buf,
                    order // 4)
    copies[5].wait()
    copies[6].wait()


def own_kernel(plan, rhs_own, inv_hi, inv_lo, perm_hi, perm_lo, top, first, second, lifted, hi_buf, lo_buf):
    leaf, place, _, _ = plan.here()
    rhs_hi, rhs_lo = split(rhs_own[...])
    lift_and_couple(rhs_hi, rhs_lo, inv_hi, inv_lo, perm_hi, perm_lo, lifted, first, second, hi_buf, lo_buf,
                    lifted.shape[0] // 2)
    for level in range(plan.levels):
        @pl.when(leaf % (plan.sharers * 2**level) == 0)
        def _():
            start = perm_hi.shape[0] - first.shape[0] + level * plan.width
            second[start : start + plan.width] += top[lanes(plan.panel(place, level), plan.width), :]


def ready_kernel(levels, top_inv, top_coup, inv, coup, back_hi, back_lo):
    width = top_inv.shape[1]
    first = 0
    for number in range(top_inv.shape[0]):
        depth = (number + 1).bit_length() - 1
        inv[number] = top_inv[number]
        turned = top_inv[number].T
        back_hi[number, :, :width], back_lo[number, :, :width] = split(turned)
        for step in range(depth):
            pair = first + step
            coup[pair] = top_coup[pair]
            columns = pl.ds((step + 1) * width, width)
            back_hi[number, :, columns], back_lo[number, :, columns] = split(
                -dot_high(turned, top_coup[pair].T))
        first += depth


def turn_kernel(inv_hi, inv_lo, perm_hi, perm_lo, lifted_own, lifted_other, base_own, base_other, gain_hi, gain_lo, token):
    hi, lo = inv_hi[...].T, inv_lo[...].T
    turned_hi, turned_lo = perm_hi[...].T, perm_lo[...].T
    gain = dot(hi, turned_hi) + (dot(hi, turned_lo) + dot(lo, turned_hi))
    gain_hi[...], gain_lo[...] = split(gain)
    base_own[...] = dot_split(hi, lo, lifted_own[...])
    base_other[...] = dot_split(hi, lo, lifted_other[...])
    token[...] = jnp.zeros_like(token)


def climb_kernel(plan, level, count, *refs):
    _, place, _, _ = plan.here()
    width = plan.width
    above = plan.levels - 1 - level
    inv, coup, forward, rest = refs[2 * count :]
    parts = [value[...] + came[...] for value, came in zip(refs[:count], refs[count : 2 * count])]
    total = jnp.concatenate(parts, 0) if count > 1 else parts[0]
    result = dot_high(inv[plan.panel(place, level)], total[:width])
    forward[...] = result
    pairs = coup[pl.ds(plan.pair(place, level, level + 1), above)]
    change = dot_high(pairs.reshape(above * width, width), result)
    rest[...] = total[width:] - change


def backward(plan, back_hi, back_lo, panel, level, forward, above):
    depth = plan.width * (plan.levels - level)
    known = jnp.concatenate([forward] + above, 0) if above else forward
    return dot_split(back_hi[panel, :, :depth], back_lo[panel, :, :depth], known)


def halve_kernel(plan, *refs):
    leaf, _, _, _ = plan.here()
    out, number = refs[-1], 0
    for ref in refs[:-1]:
        for panel in range(ref.shape[0]):
            out[number] = ref[panel, lanes(leaf % 2, plan.width // 2), :]
            number += 1


def descend_kernel(plan, *refs):
    levels, width = plan.levels, plan.width
    value, came, inv, back_hi, back_lo = refs[:5]
    forwards = refs[5 : 5 + levels - 1]
    solved = refs[5 + levels - 1]
    _, place, _, _ = plan.here()
    top = dot_high(inv[0], value[...] + came[...])
    above = []
    for level in reversed(range(levels)):
        forward = top if level == levels - 1 else forwards[level][...]
        result = backward(plan, back_hi, back_lo, plan.panel(place, level), level, forward, above)
        solved[pl.ds(level * width, width), :] = result
        above = [result] + above


def settled(base, gain_hi, gain_lo, part, column, width):
    change = dot_split(gain_hi[...], gain_lo[...], part[...])
    return base[:, column : column + width] - change


def settle_kernel(width, column, part, base, gain_hi, gain_lo, out, token):
    out[...] = settled(base, gain_hi, gain_lo, part, column, width)
    token[...] = jnp.zeros_like(token)


def last_kernel(plan, width, part, base, gain_hi, gain_lo, own, far, top, out, out_top, buffer, sems):
    _, _, core, half = plan.here()
    groups = ((1 - half) * 2 + core, half * 2 + core, (1 - half) * 2 + 1 - core, half * 2 + 1 - core)
    copies = [pltpu.make_async_copy(top, out_top, sems.at[0])]
    for done, group in zip((far, own), groups):
        copies.append(pltpu.make_async_copy(done, out.at[:, lanes(group, width)], sems.at[len(copies)]))
    for copy in copies:
        copy.start()
    known = split(jnp.concatenate([part[0], part[1]], 1))
    step = buffer.shape[0] // 2
    for start in range(0, buffer.shape[0], step):
        rows = slice(start, start + step)
        change = dot(gain_hi[rows], known[0]) + (dot(gain_hi[rows], known[1]) + dot(gain_lo[rows], known[0]))
        buffer[rows] = base[rows] - change
        for number, group in enumerate(groups[2:]):
            copies.append(pltpu.make_async_copy(
                buffer.at[pl.ds(start, step), pl.ds(number * width, width)],
                out.at[pl.ds(start, step), lanes(group, width)], sems.at[len(copies)]))
            copies[-1].start()
    for copy in copies:
        copy.wait()


def stack_place(step, level, flip):
    if level == step:
        return 2 ** (step + 1) - 2
    half = 2 ** (step - 1 - level)
    if flip < half:
        return stack_place(step - 1, level, flip)
    return 2**step - 1 + stack_place(step - 1, level, flip - half)


def top_kernel(plan, solved, back_hi, back_lo, *refs):
    levels, width = plan.levels, plan.width
    stacks, out = refs[:-1], refs[-1]
    leaf, place, _, _ = plan.here()
    second = leaf % 2 == 1
    found = {}
    for level in reversed(range(levels)):
        for flip in range(2 ** (levels - 1 - level)):
            panel = plan.panel(place, level, flip)
            if flip == 0:
                result = solved[pl.ds(level * width, width), :]
            else:
                step = flip.bit_length() - 1 + level
                number = stack_place(step, level, flip - 2 ** (step - level))
                forward = stacks[step][number]
                if step == levels - 2:
                    other = stacks[step + 1][number]
                    forward = jnp.concatenate(
                        [jnp.where(second, other, forward), jnp.where(second, forward, other)], 0)
                above = [found[up, flip >> (up - level)] for up in range(level + 1, levels)]
                result = backward(plan, back_hi, back_lo, panel, level, forward, above)
            found[level, flip] = result
            out[lanes(panel, width), :] = result


VMEM_SPEC = pl.BlockSpec(memory_space=pltpu.VMEM)
HBM_SPEC = pl.BlockSpec(memory_space=pltpu.HBM)
ANY_SPEC = pl.BlockSpec(memory_space=pl.ANY)


def call(kernel, outs, args, scratch=(), anys=(), name=None, after=(), after_hbm=(), flops=1000):
    after_hbm = [pltpu.with_memory_space_constraint(a, pltpu.HBM) for a in after_hbm]
    after_specs = [ANY_SPEC] * len(after) + [HBM_SPEC] * len(after_hbm)
    after = list(after) + after_hbm
    count = len(args)

    def body(*refs):
        kernel(*refs[:count], *refs[count + len(after) :])

    specs = [HBM_SPEC if number in anys else VMEM_SPEC for number in range(count)]
    args = [pltpu.with_memory_space_constraint(a, pltpu.HBM if number in anys else pltpu.VMEM)
            for number, a in enumerate(args)]
    return pl.pallas_call(
        body,
        out_shape=[shape for shape, _ in outs],
        in_specs=specs + after_specs,
        out_specs=[spec for _, spec in outs],
        scratch_shapes=list(scratch),
        compiler_params=pltpu.CompilerParams(vmem_limit_bytes=12 * 2**20),
        cost_estimate=pl.CostEstimate(flops=flops, bytes_accessed=1000, transcendentals=0),
        name=name,
    )(*args, *after)


def inside(shape, dtype=F32):
    return (pltpu.VMEM(shape, dtype), VMEM_SPEC)


def per_device(rhs_in, rhs_top, leaf_inv, leaf_coupling, coupling_rows, top_inv, top_coupling):
    block_count, order, _ = leaf_inv.shape
    panel_count, width, _ = top_inv.shape
    columns = rhs_top.shape[1]
    path = coupling_rows.shape[1]
    plan = Plan(lax.axis_size("leaf"), lax.axis_size("rhs"), panel_count, width)
    levels = plan.levels
    assert plan.group_count == 4 and block_count == 4 and plan.sharers >= 2

    halves = [pltpu.VMEM((order, 2 * columns), BF16)] * 2
    cut = path // 2 + 8
    pieces = [inside((cut, columns)), inside((2 * path - cut, columns))]
    sent_first, sent_second, rhs_own, lifted_other, inv_hi, inv_lo, perm_hi, perm_lo = call(
        functools.partial(lift_kernel, plan, order, columns),
        pieces + [inside((order, 2 * columns)), inside((order, 2 * columns)),
         inside((order, order), BF16), inside((order, order), BF16),
         inside((path, order), BF16), inside((path, order), BF16)],
        [rhs_in, leaf_inv, leaf_coupling, coupling_rows],
        scratch=[pltpu.VMEM((order, 2 * columns), F32), pltpu.VMEM((order, order), F32),
                 pltpu.VMEM((path, order), F32), pltpu.VMEM((1, path), jnp.int32), *halves,
                 pltpu.SemaphoreType.DMA((7,))],
        anys=(0, 1, 2, 3), name="lift")
    came_first, came_second = plan.swap_rhs(sent_first, 1), plan.swap_rhs(sent_second, 1)
    first, second, lifted_own = call(
        functools.partial(own_kernel, plan),
        pieces + [inside((order, 2 * columns))],
        [rhs_own, inv_hi, inv_lo, perm_hi, perm_lo, rhs_top], scratch=halves, name="own")
    sent = [first + came_first, second[: path - cut] + came_second[: path - cut]]
    near = second[path - cut :] + came_second[path - cut :]
    base_own, base_other, gain_hi, gain_lo, token = call(
        turn_kernel,
        [inside((order, 2 * columns)), inside((order, 2 * columns)),
         inside((order, path), BF16), inside((order, path), BF16), inside((8, columns))],
        [inv_hi, inv_lo, perm_hi, perm_lo, lifted_own, lifted_other], name="turn", after=sent)
    came = [plan.swap_rhs(part, 2) for part in sent]
    values = [near[rows] + part + token[:1] for rows, part in zip((slice(0, cut), slice(cut, path)), came)]
    backs = (panel_count, width, levels * width)
    inv, coup, back_hi, back_lo = call(
        functools.partial(ready_kernel, levels),
        [inside(top_inv.shape), inside(top_coupling.shape), inside(backs, BF16), inside(backs, BF16)],
        [top_inv, top_coupling], name="ready", after=values[1:])
    bit = 1
    while bit < plan.sharers // 2:
        values = [value + plan.swap_leaf(value, bit) for value in values]
        bit *= 2
    came = [plan.swap_leaf(value, bit) for value in values]
    value, came = values, came

    forwards, stacks, known = [], [], []
    for level in range(levels - 1):
        forward, rest = call(
            functools.partial(climb_kernel, plan, level, len(value)),
            [inside((width, columns)), inside(((levels - 1 - level) * width, columns))],
            value + came + [inv, coup], name="climb")
        bit = plan.sharers * 2**level
        value, came = [rest], [plan.swap_leaf(rest, bit)]
        forwards.append(forward)
        known = known + stacks[-1:] + [forward[None]]
        if level == levels - 2:
            stack = call(
                functools.partial(halve_kernel, plan),
                [inside((2 ** (level + 1) - 1, width // 2, columns))], known, name="halve", after=[rest])[0]
        else:
            stack = jnp.concatenate(known, 0)
        stacks.append(plan.swap_leaf(stack, bit))
    solved = call(
        functools.partial(descend_kernel, plan),
        [inside((path, columns))],
        value + came + [inv, back_hi, back_lo] + forwards, name="descend", after=stacks[:-1])[0]

    far = plan.swap_rhs(solved, 2)

    def settle(part, base, column):
        return call(
            functools.partial(settle_kernel, columns, column),
            [inside((order, columns)), inside((8, columns))],
            [part, base, gain_hi, gain_lo], name="settle")

    own, token = settle(solved, base_own, columns)
    stacks.append(plan.swap_leaf(stacks[-1] + token[:1], 1))
    pair = jnp.stack([far + token[:1], solved])
    last = plan.swap_rhs(pair, 1)
    far, token = settle(far, base_own, 0)
    top = call(
        functools.partial(top_kernel, plan),
        [inside((panel_count * width, columns))],
        [solved, back_hi, back_lo] + stacks, name="top", after=[token], flops=5 * 10**9)[0]
    out, top = call(
        functools.partial(last_kernel, plan, columns),
        [(pltpu.HBM((order, plan.group_count * columns), F32), HBM_SPEC),
         (pltpu.HBM((panel_count * width, columns), F32), HBM_SPEC)],
        [last, base_other, gain_hi, gain_lo, own, far, top],
        scratch=[pltpu.VMEM((order, 2 * columns), F32), pltpu.SemaphoreType.DMA((7,))], name="last")
    return out, top


def solution(mesh):
    placed = (
        P(("leaf", "rhs"), None),
        P(None, "rhs"),
        P("leaf", None, None),
        P("leaf", None, None),
        P("leaf", None),
        P(),
        P(),
    )
    return jax.shard_map(
        per_device,
        mesh=mesh,
        in_specs=placed,
        out_specs=(P(("leaf", "rhs"), None), P(None, "rhs")),
        check_vma=False,
    )
```

```python
import functools

import jax
import jax.numpy as jnp
from jax import lax
from jax.experimental import pallas as pl
from jax.experimental.pallas import tpu as pltpu
from jax.sharding import PartitionSpec as P

F32, BF16 = jnp.float32, jnp.bfloat16
high = lax.Precision.HIGH


def dot(left, right):
    return jnp.dot(left, right, preferred_element_type=F32)


def dot_high(left, right):
    return jnp.dot(left, right, precision=high, preferred_element_type=F32)


def split(value):
    hi = value.astype(BF16)
    return hi, (value - hi.astype(F32)).astype(BF16)


def dot_split(left_hi, left_lo, right):
    hi, lo = split(right)
    return dot(left_hi, hi) + (dot(left_hi, lo) + dot(left_lo, hi))


def lanes(number, width):
    return pl.ds(pl.multiple_of(number * width, width), width)


class Plan:
    def __init__(self, leaf_count, group_count, panel_count, width):
        self.width = width
        self.levels = (panel_count + 1).bit_length() - 1
        self.bottoms = 2 ** (self.levels - 1)
        self.leaf_count, self.group_count = leaf_count, group_count
        self.sharers = leaf_count // self.bottoms

    def here(self):
        leaf, group = lax.axis_index("leaf"), lax.axis_index("rhs")
        return leaf, leaf // self.sharers, group % 2, group // 2

    def panel(self, place, level, flip=0):
        depth = self.levels - 1 - level
        return 2**depth - 1 + ((place >> level) ^ flip)

    def swap(self, value, partner):
        pairs = []
        for leaf in range(self.leaf_count):
            for group in range(self.group_count):
                to_leaf, to_group = partner(leaf, group)
                pairs.append((leaf * self.group_count + group, to_leaf * self.group_count + to_group))
        return lax.ppermute(value, ("leaf", "rhs"), pairs)

    def swap_rhs(self, value, bit):
        return self.swap(value, lambda leaf, group: (leaf, group ^ bit))

    def swap_leaf(self, value, bit):
        return self.swap(value, lambda leaf, group: (leaf ^ bit, group))


def lift_and_couple(rhs_hi, rhs_lo, inv_hi, inv_lo, perm_hi, perm_lo, lifted, first, second, hi_buf, lo_buf, step):
    path, width = perm_hi.shape[0], first.shape[1]
    cut = first.shape[0]
    for start in range(0, lifted.shape[0], step):
        rows = slice(start, start + step)
        part = dot(inv_hi[rows], rhs_hi) + (dot(inv_hi[rows], rhs_lo) + dot(inv_lo[rows], rhs_hi))
        lifted[rows] = part
        hi_buf[rows], lo_buf[rows] = split(part)
    step = path // 2
    for start in range(0, path, step):
        rows = slice(start, start + step)
        part = dot(perm_hi[rows], hi_buf[...]) + (
            dot(perm_hi[rows], lo_buf[...]) + dot(perm_lo[rows], hi_buf[...]))
        if start < cut:
            first[start : min(start + step, cut)] = -part[: min(step, cut - start), :width]
        if start + step > cut:
            skip = max(cut - start, 0)
            second[start + skip - cut : start + step - cut] = -part[skip:, :width]
        second[path - cut + start : path - cut + start + step] = -part[:, width:]


def lift_kernel(plan, order, width, rhs, inv, coupling, rows, first, second, rhs_own, lifted, inv_hi, inv_lo,
                perm_hi, perm_lo, rhs_buf, inv_buf, coup_buf, row_buf, hi_buf, lo_buf, sems):
    _, _, core, half = plan.here()
    block = half * 2 + core
    path = coupling.shape[1]
    copies = [
        pltpu.make_async_copy(rows.at[pl.ds(block, 1)], row_buf, sems.at[0]),
        pltpu.make_async_copy(coupling.at[block], coup_buf, sems.at[1]),
    ]
    for number, side in enumerate((1 - half, half)):
        copies.append(pltpu.make_async_copy(
            rhs.at[:, lanes(side * 2 + 1 - core, width)],
            rhs_buf.at[:, pl.ds(number * width, width)], sems.at[2 + number]))
    copies.append(pltpu.make_async_copy(inv.at[block], inv_buf, sems.at[4]))
    for number, side in enumerate((1 - half, half)):
        copies.append(pltpu.make_async_copy(
            rhs.at[:, lanes(side * 2 + core, width)],
            rhs_own.at[:, pl.ds(number * width, width)], sems.at[5 + number]))
    for copy in copies:
        copy.start()
    copies[0].wait()
    chosen = (lax.broadcasted_iota(jnp.int32, (path, path), 0) == row_buf[...]).astype(BF16)
    copies[1].wait()
    coup_hi, coup_lo = split(coup_buf[...])
    perm_hi[...] = dot(chosen, coup_hi).astype(BF16)
    perm_lo[...] = dot(chosen, coup_lo).astype(BF16)
    copies[2].wait()
    copies[3].wait()
    rhs_hi, rhs_lo = split(rhs_buf[...])
    copies[4].wait()
    inv_hi[...], inv_lo[...] = split(inv_buf[...])
    lift_and_couple(rhs_hi, rhs_lo, inv_hi, inv_lo, perm_hi, perm_lo, lifted, first, second, hi_buf, lo_buf,
                    order // 4)
    copies[5].wait()
    copies[6].wait()


def own_kernel(plan, rhs_own, inv_hi, inv_lo, perm_hi, perm_lo, top, first, second, lifted, hi_buf, lo_buf):
    leaf, place, _, _ = plan.here()
    rhs_hi, rhs_lo = split(rhs_own[...])
    lift_and_couple(rhs_hi, rhs_lo, inv_hi, inv_lo, perm_hi, perm_lo, lifted, first, second, hi_buf, lo_buf,
                    lifted.shape[0] // 2)
    for level in range(plan.levels):
        @pl.when(leaf % (plan.sharers * 2**level) == 0)
        def _():
            start = perm_hi.shape[0] - first.shape[0] + level * plan.width
            second[start : start + plan.width] += top[lanes(plan.panel(place, level), plan.width), :]


def ready_kernel(top_inv, top_coup, fore_hi, fore_lo, back_hi, back_lo):
    width = top_inv.shape[1]
    first = 0
    for number in range(top_inv.shape[0]):
        depth = (number + 1).bit_length() - 1
        inv = top_inv[number]
        turned = inv.T
        fore_hi[number, :width], fore_lo[number, :width] = split(inv)
        back_hi[number, :, :width], back_lo[number, :, :width] = split(turned)
        for step in range(depth):
            change = dot_high(top_coup[first + step], inv)
            place = pl.ds((step + 1) * width, width)
            fore_hi[number, place], fore_lo[number, place] = split(change)
            back_hi[number, :, place], back_lo[number, :, place] = split(-change.T)
        first += depth


def turn_kernel(inv_hi, inv_lo, perm_hi, perm_lo, lifted_own, lifted_other, base_own, base_other, gain_hi, gain_lo, token):
    hi, lo = inv_hi[...].T, inv_lo[...].T
    turned_hi, turned_lo = perm_hi[...].T, perm_lo[...].T
    gain = dot(hi, turned_hi) + (dot(hi, turned_lo) + dot(lo, turned_hi))
    gain_hi[...], gain_lo[...] = split(gain)
    base_own[...] = dot_split(hi, lo, lifted_own[...])
    base_other[...] = dot_split(hi, lo, lifted_other[...])
    token[...] = jnp.zeros_like(token)


def climb_kernel(plan, level, count, *refs):
    _, place, _, _ = plan.here()
    width = plan.width
    above = plan.levels - 1 - level
    fore_hi, fore_lo, forward, rest = refs[2 * count :]
    parts = [value[...] + came[...] for value, came in zip(refs[:count], refs[count : 2 * count])]
    total = jnp.concatenate(parts, 0) if count > 1 else parts[0]
    panel = plan.panel(place, level)
    result = dot_split(
        fore_hi[panel, : (above + 1) * width], fore_lo[panel, : (above + 1) * width], total[:width])
    forward[...] = result[:width]
    rest[...] = total[width:] - result[width:]


def backward(plan, back_hi, back_lo, panel, level, forward, above):
    depth = plan.width * (plan.levels - level)
    known = jnp.concatenate([forward] + above, 0) if above else forward
    return dot_split(back_hi[panel, :, :depth], back_lo[panel, :, :depth], known)


def halve_kernel(plan, *refs):
    leaf, _, _, _ = plan.here()
    out, number = refs[-1], 0
    for ref in refs[:-1]:
        for panel in range(ref.shape[0]):
            out[number] = ref[panel, lanes(leaf % 2, plan.width // 2), :]
            number += 1


def descend_kernel(plan, *refs):
    levels, width = plan.levels, plan.width
    value, came, fore_hi, fore_lo, back_hi, back_lo = refs[:6]
    forwards = refs[6 : 6 + levels - 1]
    solved = refs[6 + levels - 1]
    _, place, _, _ = plan.here()
    top = dot_split(fore_hi[0, :width], fore_lo[0, :width], value[...] + came[...])
    above = []
    for level in reversed(range(levels)):
        forward = top if level == levels - 1 else forwards[level][...]
        result = backward(plan, back_hi, back_lo, plan.panel(place, level), level, forward, above)
        solved[pl.ds(level * width, width), :] = result
        above = [result] + above


def settled(base, gain_hi, gain_lo, part, column, width):
    change = dot_split(gain_hi[...], gain_lo[...], part[...])
    return base[:, column : column + width] - change


def settle_kernel(width, column, part, base, gain_hi, gain_lo, out, token):
    out[...] = settled(base, gain_hi, gain_lo, part, column, width)
    token[...] = jnp.zeros_like(token)


def last_kernel(plan, width, part, base, gain_hi, gain_lo, own, far, top, out, out_top, buffer, sems):
    _, _, core, half = plan.here()
    groups = ((1 - half) * 2 + core, half * 2 + core, (1 - half) * 2 + 1 - core, half * 2 + 1 - core)
    copies = [pltpu.make_async_copy(top, out_top, sems.at[0])]
    for done, group in zip((far, own), groups):
        copies.append(pltpu.make_async_copy(done, out.at[:, lanes(group, width)], sems.at[len(copies)]))
    for copy in copies:
        copy.start()
    known = split(jnp.concatenate([part[0], part[1]], 1))
    step = buffer.shape[0] // 2
    for start in range(0, buffer.shape[0], step):
        rows = slice(start, start + step)
        change = dot(gain_hi[rows], known[0]) + (dot(gain_hi[rows], known[1]) + dot(gain_lo[rows], known[0]))
        buffer[rows] = base[rows] - change
        for number, group in enumerate(groups[2:]):
            copies.append(pltpu.make_async_copy(
                buffer.at[pl.ds(start, step), pl.ds(number * width, width)],
                out.at[pl.ds(start, step), lanes(group, width)], sems.at[len(copies)]))
            copies[-1].start()
    for copy in copies:
        copy.wait()


def stack_place(step, level, flip):
    if level == step:
        return 2 ** (step + 1) - 2
    half = 2 ** (step - 1 - level)
    if flip < half:
        return stack_place(step - 1, level, flip)
    return 2**step - 1 + stack_place(step - 1, level, flip - half)


def top_kernel(plan, solved, back_hi, back_lo, *refs):
    levels, width = plan.levels, plan.width
    stacks, out = refs[:-1], refs[-1]
    leaf, place, _, _ = plan.here()
    second = leaf % 2 == 1
    found = {}
    for level in reversed(range(levels)):
        for flip in range(2 ** (levels - 1 - level)):
            panel = plan.panel(place, level, flip)
            if flip == 0:
                result = solved[pl.ds(level * width, width), :]
            else:
                step = flip.bit_length() - 1 + level
                number = stack_place(step, level, flip - 2 ** (step - level))
                forward = stacks[step][number]
                if step == levels - 2:
                    other = stacks[step + 1][number]
                    forward = jnp.concatenate(
                        [jnp.where(second, other, forward), jnp.where(second, forward, other)], 0)
                above = [found[up, flip >> (up - level)] for up in range(level + 1, levels)]
                result = backward(plan, back_hi, back_lo, panel, level, forward, above)
            found[level, flip] = result
            out[lanes(panel, width), :] = result


VMEM_SPEC = pl.BlockSpec(memory_space=pltpu.VMEM)
HBM_SPEC = pl.BlockSpec(memory_space=pltpu.HBM)
ANY_SPEC = pl.BlockSpec(memory_space=pl.ANY)


def call(kernel, outs, args, scratch=(), anys=(), name=None, after=(), after_hbm=(), flops=1000):
    after_hbm = [pltpu.with_memory_space_constraint(a, pltpu.HBM) for a in after_hbm]
    after_specs = [ANY_SPEC] * len(after) + [HBM_SPEC] * len(after_hbm)
    after = list(after) + after_hbm
    count = len(args)

    def body(*refs):
        kernel(*refs[:count], *refs[count + len(after) :])

    specs = [HBM_SPEC if number in anys else VMEM_SPEC for number in range(count)]
    args = [pltpu.with_memory_space_constraint(a, pltpu.HBM if number in anys else pltpu.VMEM)
            for number, a in enumerate(args)]
    return pl.pallas_call(
        body,
        out_shape=[shape for shape, _ in outs],
        in_specs=specs + after_specs,
        out_specs=[spec for _, spec in outs],
        scratch_shapes=list(scratch),
        compiler_params=pltpu.CompilerParams(vmem_limit_bytes=12 * 2**20),
        cost_estimate=pl.CostEstimate(flops=flops, bytes_accessed=1000, transcendentals=0),
        name=name,
    )(*args, *after)


def inside(shape, dtype=F32):
    return (pltpu.VMEM(shape, dtype), VMEM_SPEC)


def per_device(rhs_in, rhs_top, leaf_inv, leaf_coupling, coupling_rows, top_inv, top_coupling):
    block_count, order, _ = leaf_inv.shape
    panel_count, width, _ = top_inv.shape
    columns = rhs_top.shape[1]
    path = coupling_rows.shape[1]
    plan = Plan(lax.axis_size("leaf"), lax.axis_size("rhs"), panel_count, width)
    levels = plan.levels
    assert plan.group_count == 4 and block_count == 4 and plan.sharers >= 2

    halves = [pltpu.VMEM((order, 2 * columns), BF16)] * 2
    cut = path // 2 + 8
    pieces = [inside((cut, columns)), inside((2 * path - cut, columns))]
    sent_first, sent_second, rhs_own, lifted_other, inv_hi, inv_lo, perm_hi, perm_lo = call(
        functools.partial(lift_kernel, plan, order, columns),
        pieces + [inside((order, 2 * columns)), inside((order, 2 * columns)),
         inside((order, order), BF16), inside((order, order), BF16),
         inside((path, order), BF16), inside((path, order), BF16)],
        [rhs_in, leaf_inv, leaf_coupling, coupling_rows],
        scratch=[pltpu.VMEM((order, 2 * columns), F32), pltpu.VMEM((order, order), F32),
                 pltpu.VMEM((path, order), F32), pltpu.VMEM((1, path), jnp.int32), *halves,
                 pltpu.SemaphoreType.DMA((7,))],
        anys=(0, 1, 2, 3), name="lift")
    came_first, came_second = plan.swap_rhs(sent_first, 1), plan.swap_rhs(sent_second, 1)
    first, second, lifted_own = call(
        functools.partial(own_kernel, plan),
        pieces + [inside((order, 2 * columns))],
        [rhs_own, inv_hi, inv_lo, perm_hi, perm_lo, rhs_top], scratch=halves, name="own")
    sent = [first + came_first, second[: path - cut] + came_second[: path - cut]]
    near = second[path - cut :] + came_second[path - cut :]
    base_own, base_other, gain_hi, gain_lo, token = call(
        turn_kernel,
        [inside((order, 2 * columns)), inside((order, 2 * columns)),
         inside((order, path), BF16), inside((order, path), BF16), inside((8, columns))],
        [inv_hi, inv_lo, perm_hi, perm_lo, lifted_own, lifted_other], name="turn", after=sent)
    came = [plan.swap_rhs(part, 2) for part in sent]
    values = [near[rows] + part + token[:1] for rows, part in zip((slice(0, cut), slice(cut, path)), came)]
    fores, backs = (panel_count, levels * width, width), (panel_count, width, levels * width)
    fore_hi, fore_lo, back_hi, back_lo = call(
        ready_kernel,
        [inside(fores, BF16), inside(fores, BF16), inside(backs, BF16), inside(backs, BF16)],
        [top_inv, top_coupling], name="ready", after=values[1:])
    bit = 1
    while bit < plan.sharers // 2:
        values = [value + plan.swap_leaf(value, bit) for value in values]
        bit *= 2
    came = [plan.swap_leaf(value, bit) for value in values]
    value, came = values, came

    forwards, stacks, known = [], [], []
    for level in range(levels - 1):
        forward, rest = call(
            functools.partial(climb_kernel, plan, level, len(value)),
            [inside((width, columns)), inside(((levels - 1 - level) * width, columns))],
            value + came + [fore_hi, fore_lo], name="climb")
        bit = plan.sharers * 2**level
        value, came = [rest], [plan.swap_leaf(rest, bit)]
        forwards.append(forward)
        known = known + stacks[-1:] + [forward[None]]
        if level == levels - 2:
            stack = call(
                functools.partial(halve_kernel, plan),
                [inside((2 ** (level + 1) - 1, width // 2, columns))], known, name="halve", after=[rest])[0]
        else:
            stack = jnp.concatenate(known, 0)
        stacks.append(plan.swap_leaf(stack, bit))
    solved = call(
        functools.partial(descend_kernel, plan),
        [inside((path, columns))],
        value + came + [fore_hi, fore_lo, back_hi, back_lo] + forwards, name="descend", after=stacks[:-1])[0]

    far = plan.swap_rhs(solved, 2)

    def settle(part, base, column):
        return call(
            functools.partial(settle_kernel, columns, column),
            [inside((order, columns)), inside((8, columns))],
            [part, base, gain_hi, gain_lo], name="settle")

    own, token = settle(solved, base_own, columns)
    stacks.append(plan.swap_leaf(stacks[-1] + token[:1], 1))
    pair = jnp.stack([far + token[:1], solved])
    last = plan.swap_rhs(pair, 1)
    far, token = settle(far, base_own, 0)
    top = call(
        functools.partial(top_kernel, plan),
        [inside((panel_count * width, columns))],
        [solved, back_hi, back_lo] + stacks, name="top", after=[token], flops=5 * 10**9)[0]
    out, top = call(
        functools.partial(last_kernel, plan, columns),
        [(pltpu.HBM((order, plan.group_count * columns), F32), HBM_SPEC),
         (pltpu.HBM((panel_count * width, columns), F32), HBM_SPEC)],
        [last, base_other, gain_hi, gain_lo, own, far, top],
        scratch=[pltpu.VMEM((order, 2 * columns), F32), pltpu.SemaphoreType.DMA((7,))], name="last")
    return out, top


def solution(mesh):
    placed = (
        P(("leaf", "rhs"), None),
        P(None, "rhs"),
        P("leaf", None, None),
        P("leaf", None, None),
        P("leaf", None),
        P(),
        P(),
    )
    return jax.shard_map(
        per_device,
        mesh=mesh,
        in_specs=placed,
        out_specs=(P(("leaf", "rhs"), None), P(None, "rhs")),
        check_vma=False,
    )
```

```python
import functools

import jax
import jax.numpy as jnp
from jax import lax
from jax.experimental import pallas as pl
from jax.experimental.pallas import tpu as pltpu
from jax.sharding import PartitionSpec as P

F32, BF16 = jnp.float32, jnp.bfloat16
high = lax.Precision.HIGH


def dot(left, right):
    return jnp.dot(left, right, preferred_element_type=F32)


def dot_high(left, right):
    return jnp.dot(left, right, precision=high, preferred_element_type=F32)


def split(value):
    hi = value.astype(BF16)
    return hi, (value - hi.astype(F32)).astype(BF16)


def dot_split(left_hi, left_lo, right):
    hi, lo = split(right)
    return dot(left_hi, hi) + (dot(left_hi, lo) + dot(left_lo, hi))


def lanes(number, width):
    return pl.ds(pl.multiple_of(number * width, width), width)


class Plan:
    def __init__(self, leaf_count, group_count, panel_count, width):
        self.width = width
        self.levels = (panel_count + 1).bit_length() - 1
        self.bottoms = 2 ** (self.levels - 1)
        self.leaf_count, self.group_count = leaf_count, group_count
        self.sharers = leaf_count // self.bottoms

    def here(self):
        leaf, group = lax.axis_index("leaf"), lax.axis_index("rhs")
        return leaf, leaf // self.sharers, group % 2, group // 2

    def panel(self, place, level, flip=0):
        depth = self.levels - 1 - level
        return 2**depth - 1 + ((place >> level) ^ flip)

    def swap(self, value, partner):
        pairs = []
        for leaf in range(self.leaf_count):
            for group in range(self.group_count):
                to_leaf, to_group = partner(leaf, group)
                pairs.append((leaf * self.group_count + group, to_leaf * self.group_count + to_group))
        return lax.ppermute(value, ("leaf", "rhs"), pairs)

    def swap_rhs(self, value, bit):
        return self.swap(value, lambda leaf, group: (leaf, group ^ bit))

    def swap_leaf(self, value, bit):
        return self.swap(value, lambda leaf, group: (leaf ^ bit, group))


def lift_and_couple(rhs_hi, rhs_lo, inv_hi, inv_lo, perm_hi, perm_lo, lifted, first, second, hi_buf, lo_buf, step):
    path, width = perm_hi.shape[0], first.shape[1]
    cut = first.shape[0]
    for start in range(0, lifted.shape[0], step):
        rows = slice(start, start + step)
        part = dot(inv_hi[rows], rhs_hi) + (dot(inv_hi[rows], rhs_lo) + dot(inv_lo[rows], rhs_hi))
        lifted[rows] = part
        hi_buf[rows], lo_buf[rows] = split(part)
    step = path // 2
    for start in range(0, path, step):
        rows = slice(start, start + step)
        part = dot(perm_hi[rows], hi_buf[...]) + (
            dot(perm_hi[rows], lo_buf[...]) + dot(perm_lo[rows], hi_buf[...]))
        if start < cut:
            first[start : min(start + step, cut)] = -part[: min(step, cut - start), :width]
        if start + step > cut:
            skip = max(cut - start, 0)
            second[start + skip - cut : start + step - cut] = -part[skip:, :width]
        second[path - cut + start : path - cut + start + step] = -part[:, width:]


def lift_kernel(plan, order, width, rhs, inv, coupling, rows, first, second, rhs_own, lifted, inv_hi, inv_lo,
                perm_hi, perm_lo, rhs_buf, inv_buf, coup_buf, row_buf, hi_buf, lo_buf, sems):
    _, _, core, half = plan.here()
    block = half * 2 + core
    path = coupling.shape[1]
    copies = [
        pltpu.make_async_copy(rows.at[pl.ds(block, 1)], row_buf, sems.at[0]),
        pltpu.make_async_copy(coupling.at[block], coup_buf, sems.at[1]),
    ]
    for number, side in enumerate((1 - half, half)):
        copies.append(pltpu.make_async_copy(
            rhs.at[:, lanes(side * 2 + 1 - core, width)],
            rhs_buf.at[:, pl.ds(number * width, width)], sems.at[2 + number]))
    copies.append(pltpu.make_async_copy(inv.at[block], inv_buf, sems.at[4]))
    for number, side in enumerate((1 - half, half)):
        copies.append(pltpu.make_async_copy(
            rhs.at[:, lanes(side * 2 + core, width)],
            rhs_own.at[:, pl.ds(number * width, width)], sems.at[5 + number]))
    for copy in copies:
        copy.start()
    copies[0].wait()
    chosen = (lax.broadcasted_iota(jnp.int32, (path, path), 0) == row_buf[...]).astype(BF16)
    copies[1].wait()
    coup_hi, coup_lo = split(coup_buf[...])
    perm_hi[...] = dot(chosen, coup_hi).astype(BF16)
    perm_lo[...] = dot(chosen, coup_lo).astype(BF16)
    copies[2].wait()
    copies[3].wait()
    rhs_hi, rhs_lo = split(rhs_buf[...])
    copies[4].wait()
    inv_hi[...], inv_lo[...] = split(inv_buf[...])
    lift_and_couple(rhs_hi, rhs_lo, inv_hi, inv_lo, perm_hi, perm_lo, lifted, first, second, hi_buf, lo_buf,
                    order // 4)
    copies[5].wait()
    copies[6].wait()


def own_kernel(plan, rhs_own, inv_hi, inv_lo, perm_hi, perm_lo, top, first, second, lifted, hi_buf, lo_buf):
    leaf, place, _, _ = plan.here()
    rhs_hi, rhs_lo = split(rhs_own[...])
    lift_and_couple(rhs_hi, rhs_lo, inv_hi, inv_lo, perm_hi, perm_lo, lifted, first, second, hi_buf, lo_buf,
                    lifted.shape[0] // 2)
    for level in range(plan.levels):
        @pl.when(leaf % (plan.sharers * 2**level) == 0)
        def _():
            start = perm_hi.shape[0] - first.shape[0] + level * plan.width
            second[start : start + plan.width] += top[lanes(plan.panel(place, level), plan.width), :]


def ready_kernel(top_inv, top_coup, fore_hi, fore_lo, back_hi, back_lo):
    width = top_inv.shape[1]
    first = 0
    for number in range(top_inv.shape[0]):
        depth = (number + 1).bit_length() - 1
        inv = top_inv[number]
        turned = inv.T
        fore_hi[number, :width], fore_lo[number, :width] = split(inv)
        back_hi[number, :, :width], back_lo[number, :, :width] = split(turned)
        for step in range(depth):
            change = dot_high(top_coup[first + step], inv)
            place = pl.ds((step + 1) * width, width)
            fore_hi[number, place], fore_lo[number, place] = split(change)
            back_hi[number, :, place], back_lo[number, :, place] = split(-change.T)
        first += depth


def turn_kernel(inv_hi, inv_lo, perm_hi, perm_lo, lifted_own, lifted_other, base_own, base_other, gain_hi, gain_lo, token):
    hi, lo = inv_hi[...].T, inv_lo[...].T
    turned_hi, turned_lo = perm_hi[...].T, perm_lo[...].T
    gain = dot(hi, turned_hi) + (dot(hi, turned_lo) + dot(lo, turned_hi))
    gain_hi[...], gain_lo[...] = split(gain)
    base_own[...] = dot_split(hi, lo, lifted_own[...])
    base_other[...] = dot_split(hi, lo, lifted_other[...])
    token[...] = jnp.zeros_like(token)


def climb_kernel(plan, level, count, *refs):
    _, place, _, _ = plan.here()
    width = plan.width
    above = plan.levels - 1 - level
    fore_hi, fore_lo, forward, rest = refs[2 * count :]
    parts = [value[...] + came[...] for value, came in zip(refs[:count], refs[count : 2 * count])]
    total = jnp.concatenate(parts, 0) if count > 1 else parts[0]
    panel = plan.panel(place, level)
    result = dot_split(
        fore_hi[panel, : (above + 1) * width], fore_lo[panel, : (above + 1) * width], total[:width])
    forward[...] = result[:width]
    rest[...] = total[width:] - result[width:]


def backward(plan, back_hi, back_lo, panel, level, forward, above):
    depth = plan.width * (plan.levels - level)
    known = jnp.concatenate([forward] + above, 0) if above else forward
    return dot_split(back_hi[panel, :, :depth], back_lo[panel, :, :depth], known)


def halve_kernel(plan, *refs):
    leaf, _, _, _ = plan.here()
    out, number = refs[-1], 0
    for ref in refs[:-1]:
        for panel in range(ref.shape[0]):
            out[number] = ref[panel, lanes(leaf % 2, plan.width // 2), :]
            number += 1


def descend_kernel(plan, *refs):
    levels, width = plan.levels, plan.width
    value, came, fore_hi, fore_lo, back_hi, back_lo = refs[:6]
    forwards = refs[6 : 6 + levels - 1]
    solved = refs[6 + levels - 1]
    _, place, _, _ = plan.here()
    top = dot_split(fore_hi[0, :width], fore_lo[0, :width], value[...] + came[...])
    above = []
    for level in reversed(range(levels)):
        forward = top if level == levels - 1 else forwards[level][...]
        result = backward(plan, back_hi, back_lo, plan.panel(place, level), level, forward, above)
        solved[pl.ds(level * width, width), :] = result
        above = [result] + above


def settled(base, gain_hi, gain_lo, part, column, width):
    change = dot_split(gain_hi[...], gain_lo[...], part[...])
    return base[:, column : column + width] - change


def settle_kernel(width, column, part, base, gain_hi, gain_lo, out, token):
    out[...] = settled(base, gain_hi, gain_lo, part, column, width)
    token[...] = jnp.zeros_like(token)


def last_kernel(plan, width, part, base, gain_hi, gain_lo, far, own, cross, top, out, out_top, buffer, sems):
    _, _, core, half = plan.here()
    groups = ((1 - half) * 2 + core, half * 2 + core, half * 2 + 1 - core, (1 - half) * 2 + 1 - core)
    copies = [pltpu.make_async_copy(top, out_top, sems.at[0])]
    for done, group in zip((far, own, cross), groups):
        copies.append(pltpu.make_async_copy(done, out.at[:, lanes(group, width)], sems.at[len(copies)]))
    for copy in copies:
        copy.start()
    known = split(part[...])
    step = buffer.shape[0] // 2
    for start in range(0, buffer.shape[0], step):
        rows = slice(start, start + step)
        change = dot(gain_hi[rows], known[0]) + (dot(gain_hi[rows], known[1]) + dot(gain_lo[rows], known[0]))
        buffer[rows] = base[rows, :width] - change
        copies.append(pltpu.make_async_copy(
            buffer.at[pl.ds(start, step)], out.at[pl.ds(start, step), lanes(groups[3], width)],
            sems.at[len(copies)]))
        copies[-1].start()
    for copy in copies:
        copy.wait()


def stack_place(step, level, flip):
    if level == step:
        return 2 ** (step + 1) - 2
    half = 2 ** (step - 1 - level)
    if flip < half:
        return stack_place(step - 1, level, flip)
    return 2**step - 1 + stack_place(step - 1, level, flip - half)


def top_kernel(plan, solved, back_hi, back_lo, *refs):
    levels, width = plan.levels, plan.width
    stacks, out = refs[:-1], refs[-1]
    leaf, place, _, _ = plan.here()
    second = leaf % 2 == 1
    found = {}
    for level in reversed(range(levels)):
        for flip in range(2 ** (levels - 1 - level)):
            panel = plan.panel(place, level, flip)
            if flip == 0:
                result = solved[pl.ds(level * width, width), :]
            else:
                step = flip.bit_length() - 1 + level
                number = stack_place(step, level, flip - 2 ** (step - level))
                forward = stacks[step][number]
                if step == levels - 2:
                    other = stacks[step + 1][number]
                    forward = jnp.concatenate(
                        [jnp.where(second, other, forward), jnp.where(second, forward, other)], 0)
                above = [found[up, flip >> (up - level)] for up in range(level + 1, levels)]
                result = backward(plan, back_hi, back_lo, panel, level, forward, above)
            found[level, flip] = result
            out[lanes(panel, width), :] = result


VMEM_SPEC = pl.BlockSpec(memory_space=pltpu.VMEM)
HBM_SPEC = pl.BlockSpec(memory_space=pltpu.HBM)
ANY_SPEC = pl.BlockSpec(memory_space=pl.ANY)


def call(kernel, outs, args, scratch=(), anys=(), name=None, after=(), after_hbm=(), flops=1000):
    after_hbm = [pltpu.with_memory_space_constraint(a, pltpu.HBM) for a in after_hbm]
    after_specs = [ANY_SPEC] * len(after) + [HBM_SPEC] * len(after_hbm)
    after = list(after) + after_hbm
    count = len(args)

    def body(*refs):
        kernel(*refs[:count], *refs[count + len(after) :])

    specs = [HBM_SPEC if number in anys else VMEM_SPEC for number in range(count)]
    args = [pltpu.with_memory_space_constraint(a, pltpu.HBM if number in anys else pltpu.VMEM)
            for number, a in enumerate(args)]
    return pl.pallas_call(
        body,
        out_shape=[shape for shape, _ in outs],
        in_specs=specs + after_specs,
        out_specs=[spec for _, spec in outs],
        scratch_shapes=list(scratch),
        compiler_params=pltpu.CompilerParams(vmem_limit_bytes=12 * 2**20),
        cost_estimate=pl.CostEstimate(flops=flops, bytes_accessed=1000, transcendentals=0),
        name=name,
    )(*args, *after)


def inside(shape, dtype=F32):
    return (pltpu.VMEM(shape, dtype), VMEM_SPEC)


def per_device(rhs_in, rhs_top, leaf_inv, leaf_coupling, coupling_rows, top_inv, top_coupling):
    block_count, order, _ = leaf_inv.shape
    panel_count, width, _ = top_inv.shape
    columns = rhs_top.shape[1]
    path = coupling_rows.shape[1]
    plan = Plan(lax.axis_size("leaf"), lax.axis_size("rhs"), panel_count, width)
    levels = plan.levels
    assert plan.group_count == 4 and block_count == 4 and plan.sharers >= 2

    halves = [pltpu.VMEM((order, 2 * columns), BF16)] * 2
    cut = path // 2 + 32
    pieces = [inside((cut, columns)), inside((2 * path - cut, columns))]
    sent_first, sent_second, rhs_own, lifted_other, inv_hi, inv_lo, perm_hi, perm_lo = call(
        functools.partial(lift_kernel, plan, order, columns),
        pieces + [inside((order, 2 * columns)), inside((order, 2 * columns)),
         inside((order, order), BF16), inside((order, order), BF16),
         inside((path, order), BF16), inside((path, order), BF16)],
        [rhs_in, leaf_inv, leaf_coupling, coupling_rows],
        scratch=[pltpu.VMEM((order, 2 * columns), F32), pltpu.VMEM((order, order), F32),
                 pltpu.VMEM((path, order), F32), pltpu.VMEM((1, path), jnp.int32), *halves,
                 pltpu.SemaphoreType.DMA((7,))],
        anys=(0, 1, 2, 3), name="lift")
    came_first, came_second = plan.swap_rhs(sent_first, 1), plan.swap_rhs(sent_second, 1)
    first, second, lifted_own = call(
        functools.partial(own_kernel, plan),
        pieces + [inside((order, 2 * columns))],
        [rhs_own, inv_hi, inv_lo, perm_hi, perm_lo, rhs_top], scratch=halves, name="own")
    sent = [first + came_first, second[: path - cut] + came_second[: path - cut]]
    near = second[path - cut :] + came_second[path - cut :]
    base_own, base_other, gain_hi, gain_lo, token = call(
        turn_kernel,
        [inside((order, 2 * columns)), inside((order, 2 * columns)),
         inside((order, path), BF16), inside((order, path), BF16), inside((8, columns))],
        [inv_hi, inv_lo, perm_hi, perm_lo, lifted_own, lifted_other], name="turn", after=sent)
    came = [plan.swap_rhs(part, 2) for part in sent]
    values = [near[rows] + part + token[:1] for rows, part in zip((slice(0, cut), slice(cut, path)), came)]
    fores, backs = (panel_count, levels * width, width), (panel_count, width, levels * width)
    fore_hi, fore_lo, back_hi, back_lo = call(
        ready_kernel,
        [inside(fores, BF16), inside(fores, BF16), inside(backs, BF16), inside(backs, BF16)],
        [top_inv, top_coupling], name="ready", after=values[1:])
    bit = 1
    while bit < plan.sharers // 2:
        values = [value + plan.swap_leaf(value, bit) for value in values]
        bit *= 2
    came = [plan.swap_leaf(value, bit) for value in values]
    value, came = values, came

    forwards, stacks, known = [], [], []
    for level in range(levels - 1):
        forward, rest = call(
            functools.partial(climb_kernel, plan, level, len(value)),
            [inside((width, columns)), inside(((levels - 1 - level) * width, columns))],
            value + came + [fore_hi, fore_lo], name="climb")
        bit = plan.sharers * 2**level
        value, came = [rest], [plan.swap_leaf(rest, bit)]
        forwards.append(forward)
        known = known + stacks[-1:] + [forward[None]]
        if level == levels - 2:
            stack = call(
                functools.partial(halve_kernel, plan),
                [inside((2 ** (level + 1) - 1, width // 2, columns))], known, name="halve", after=[rest])[0]
        else:
            stack = jnp.concatenate(known, 0)
        stacks.append(plan.swap_leaf(stack, bit))
    solved = call(
        functools.partial(descend_kernel, plan),
        [inside((path, columns))],
        value + came + [fore_hi, fore_lo, back_hi, back_lo] + forwards, name="descend", after=stacks[:-1])[0]

    far = plan.swap_rhs(solved, 2)

    def settle(part, base, column):
        return call(
            functools.partial(settle_kernel, columns, column),
            [inside((order, columns)), inside((8, columns))],
            [part, base, gain_hi, gain_lo], name="settle")

    own, token = settle(solved, base_own, columns)
    cross = plan.swap_rhs(solved + token[:1], 1)
    stacks.append(plan.swap_leaf(stacks[-1] + token[:1], 1))
    cross, token = settle(cross, base_other, columns)
    far = far + token[:1]
    last = plan.swap_rhs(far, 1)
    far, token = settle(far, base_own, 0)
    top = call(
        functools.partial(top_kernel, plan),
        [inside((panel_count * width, columns))],
        [solved, back_hi, back_lo] + stacks, name="top", after=[token], flops=5 * 10**9)[0]
    out, top = call(
        functools.partial(last_kernel, plan, columns),
        [(pltpu.HBM((order, plan.group_count * columns), F32), HBM_SPEC),
         (pltpu.HBM((panel_count * width, columns), F32), HBM_SPEC)],
        [last, base_other, gain_hi, gain_lo, far, own, cross, top],
        scratch=[pltpu.VMEM((order, columns), F32), pltpu.SemaphoreType.DMA((6,))], name="last")
    return out, top


def solution(mesh):
    placed = (
        P(("leaf", "rhs"), None),
        P(None, "rhs"),
        P("leaf", None, None),
        P("leaf", None, None),
        P("leaf", None),
        P(),
        P(),
    )
    return jax.shard_map(
        per_device,
        mesh=mesh,
        in_specs=placed,
        out_specs=(P(("leaf", "rhs"), None), P(None, "rhs")),
        check_vma=False,
    )
```

```python
import functools

import jax
import jax.numpy as jnp
from jax import lax
from jax.experimental import pallas as pl
from jax.experimental.pallas import tpu as pltpu
from jax.sharding import PartitionSpec as P

F32, BF16 = jnp.float32, jnp.bfloat16
high = lax.Precision.HIGH


def dot(left, right):
    return jnp.dot(left, right, preferred_element_type=F32)


def dot_high(left, right):
    return jnp.dot(left, right, precision=high, preferred_element_type=F32)


def split(value):
    hi = value.astype(BF16)
    return hi, (value - hi.astype(F32)).astype(BF16)


def dot_split(left_hi, left_lo, right):
    hi, lo = split(right)
    return dot(left_hi, hi) + (dot(left_hi, lo) + dot(left_lo, hi))


def lanes(number, width):
    return pl.ds(pl.multiple_of(number * width, width), width)


class Plan:
    def __init__(self, leaf_count, group_count, panel_count, width):
        self.width = width
        self.levels = (panel_count + 1).bit_length() - 1
        self.bottoms = 2 ** (self.levels - 1)
        self.leaf_count, self.group_count = leaf_count, group_count
        self.sharers = leaf_count // self.bottoms

    def here(self):
        leaf, group = lax.axis_index("leaf"), lax.axis_index("rhs")
        return leaf, leaf // self.sharers, group % 2, group // 2

    def panel(self, place, level, flip=0):
        depth = self.levels - 1 - level
        return 2**depth - 1 + ((place >> level) ^ flip)

    def swap(self, value, partner):
        pairs = []
        for leaf in range(self.leaf_count):
            for group in range(self.group_count):
                to_leaf, to_group = partner(leaf, group)
                pairs.append((leaf * self.group_count + group, to_leaf * self.group_count + to_group))
        return lax.ppermute(value, ("leaf", "rhs"), pairs)

    def swap_rhs(self, value, bit):
        return self.swap(value, lambda leaf, group: (leaf, group ^ bit))

    def swap_leaf(self, value, bit):
        return self.swap(value, lambda leaf, group: (leaf ^ bit, group))


def lift_and_couple(rhs_hi, rhs_lo, inv_hi, inv_lo, perm_hi, perm_lo, lifted, first, second, hi_buf, lo_buf, step):
    path, width = perm_hi.shape[0], first.shape[1]
    cut = first.shape[0]
    for start in range(0, lifted.shape[0], step):
        rows = slice(start, start + step)
        part = dot(inv_hi[rows], rhs_hi) + (dot(inv_hi[rows], rhs_lo) + dot(inv_lo[rows], rhs_hi))
        lifted[rows] = part
        hi_buf[rows], lo_buf[rows] = split(part)
    step = path // 2
    for start in range(0, path, step):
        rows = slice(start, start + step)
        part = dot(perm_hi[rows], hi_buf[...]) + (
            dot(perm_hi[rows], lo_buf[...]) + dot(perm_lo[rows], hi_buf[...]))
        if start < cut:
            first[start : min(start + step, cut)] = -part[: min(step, cut - start), :width]
        if start + step > cut:
            skip = max(cut - start, 0)
            second[start + skip - cut : start + step - cut] = -part[skip:, :width]
        second[path - cut + start : path - cut + start + step] = -part[:, width:]


def lift_kernel(plan, order, width, rhs, inv, coupling, rows, first, second, rhs_own, lifted, inv_hi, inv_lo,
                perm_hi, perm_lo, rhs_buf, inv_buf, coup_buf, row_buf, hi_buf, lo_buf, sems):
    _, _, core, half = plan.here()
    block = half * 2 + core
    path = coupling.shape[1]
    copies = [
        pltpu.make_async_copy(rows.at[pl.ds(block, 1)], row_buf, sems.at[0]),
        pltpu.make_async_copy(coupling.at[block], coup_buf, sems.at[1]),
    ]
    for number, side in enumerate((1 - half, half)):
        copies.append(pltpu.make_async_copy(
            rhs.at[:, lanes(side * 2 + 1 - core, width)],
            rhs_buf.at[:, pl.ds(number * width, width)], sems.at[2 + number]))
    copies.append(pltpu.make_async_copy(inv.at[block], inv_buf, sems.at[4]))
    for number, side in enumerate((1 - half, half)):
        copies.append(pltpu.make_async_copy(
            rhs.at[:, lanes(side * 2 + core, width)],
            rhs_own.at[:, pl.ds(number * width, width)], sems.at[5 + number]))
    for copy in copies:
        copy.start()
    copies[0].wait()
    chosen = (lax.broadcasted_iota(jnp.int32, (path, path), 0) == row_buf[...]).astype(BF16)
    copies[1].wait()
    coup_hi, coup_lo = split(coup_buf[...])
    perm_hi[...] = dot(chosen, coup_hi).astype(BF16)
    perm_lo[...] = dot(chosen, coup_lo).astype(BF16)
    copies[2].wait()
    copies[3].wait()
    rhs_hi, rhs_lo = split(rhs_buf[...])
    copies[4].wait()
    inv_hi[...], inv_lo[...] = split(inv_buf[...])
    lift_and_couple(rhs_hi, rhs_lo, inv_hi, inv_lo, perm_hi, perm_lo, lifted, first, second, hi_buf, lo_buf,
                    order // 4)
    copies[5].wait()
    copies[6].wait()


def own_kernel(plan, rhs_own, inv_hi, inv_lo, perm_hi, perm_lo, top, first, second, lifted, hi_buf, lo_buf):
    leaf, place, _, _ = plan.here()
    rhs_hi, rhs_lo = split(rhs_own[...])
    lift_and_couple(rhs_hi, rhs_lo, inv_hi, inv_lo, perm_hi, perm_lo, lifted, first, second, hi_buf, lo_buf,
                    lifted.shape[0] // 2)
    for level in range(plan.levels):
        @pl.when(leaf % (plan.sharers * 2**level) == 0)
        def _():
            start = perm_hi.shape[0] - first.shape[0] + level * plan.width
            second[start : start + plan.width] += top[lanes(plan.panel(place, level), plan.width), :]


def ready_kernel(top_inv, top_coup, fore_hi, fore_lo, back_hi, back_lo):
    width = top_inv.shape[1]
    first = 0
    for number in range(top_inv.shape[0]):
        depth = (number + 1).bit_length() - 1
        inv = top_inv[number]
        turned = inv.T
        fore_hi[number, :width], fore_lo[number, :width] = split(inv)
        back_hi[number, :, :width], back_lo[number, :, :width] = split(turned)
        for step in range(depth):
            change = dot_high(top_coup[first + step], inv)
            place = pl.ds((step + 1) * width, width)
            fore_hi[number, place], fore_lo[number, place] = split(change)
            back_hi[number, :, place], back_lo[number, :, place] = split(-change.T)
        first += depth


def turn_kernel(inv_hi, inv_lo, perm_hi, perm_lo, lifted_own, lifted_other, base_own, base_other, gain_hi, gain_lo, token):
    hi, lo = inv_hi[...].T, inv_lo[...].T
    turned_hi, turned_lo = perm_hi[...].T, perm_lo[...].T
    gain = dot(hi, turned_hi) + (dot(hi, turned_lo) + dot(lo, turned_hi))
    gain_hi[...], gain_lo[...] = split(gain)
    base_own[...] = dot_split(hi, lo, lifted_own[...])
    base_other[...] = dot_split(hi, lo, lifted_other[...])
    token[...] = jnp.zeros_like(token)


def climb_kernel(plan, level, count, *refs):
    _, place, _, _ = plan.here()
    width = plan.width
    above = plan.levels - 1 - level
    fore_hi, fore_lo, forward, rest = refs[2 * count :]
    parts = [value[...] + came[...] for value, came in zip(refs[:count], refs[count : 2 * count])]
    total = jnp.concatenate(parts, 0) if count > 1 else parts[0]
    panel = plan.panel(place, level)
    result = dot_split(
        fore_hi[panel, : (above + 1) * width], fore_lo[panel, : (above + 1) * width], total[:width])
    forward[...] = result[:width]
    rest[...] = total[width:] - result[width:]


def backward(plan, back_hi, back_lo, panel, level, forward, above):
    depth = plan.width * (plan.levels - level)
    known = jnp.concatenate([forward] + above, 0) if above else forward
    return dot_split(back_hi[panel, :, :depth], back_lo[panel, :, :depth], known)


def halve_kernel(plan, *refs):
    leaf, _, _, _ = plan.here()
    out, number = refs[-1], 0
    for ref in refs[:-1]:
        for panel in range(ref.shape[0]):
            out[number] = ref[panel, lanes(leaf % 2, plan.width // 2), :]
            number += 1


def descend_kernel(plan, *refs):
    levels, width = plan.levels, plan.width
    value, came, fore_hi, fore_lo, back_hi, back_lo = refs[:6]
    forwards = refs[6 : 6 + levels - 1]
    solved = refs[6 + levels - 1]
    _, place, _, _ = plan.here()
    top = dot_split(fore_hi[0, :width], fore_lo[0, :width], value[...] + came[...])
    above = []
    for level in reversed(range(levels)):
        forward = top if level == levels - 1 else forwards[level][...]
        result = backward(plan, back_hi, back_lo, plan.panel(place, level), level, forward, above)
        solved[pl.ds(level * width, width), :] = result
        above = [result] + above


def settled(base, gain_hi, gain_lo, part, column, width):
    change = dot_split(gain_hi[...], gain_lo[...], part[...])
    return base[:, column : column + width] - change


def settle_kernel(width, column, part, base, gain_hi, gain_lo, out, token):
    out[...] = settled(base, gain_hi, gain_lo, part, column, width)
    token[...] = jnp.zeros_like(token)


def cross_kernel(plan, width, column, part, base, gain_hi, gain_lo, own, out, token, buffer, sems):
    _, _, core, half = plan.here()
    copies = [pltpu.make_async_copy(own, out.at[:, lanes(half * 2 + core, width)], sems.at[0]),
              pltpu.make_async_copy(buffer, out.at[:, lanes(half * 2 + 1 - core, width)], sems.at[1])]
    copies[0].start()
    buffer[...] = settled(base, gain_hi, gain_lo, part, column, width)
    copies[1].start()
    token[...] = jnp.zeros_like(token)
    for copy in copies:
        copy.wait()


def last_kernel(plan, width, part, base, gain_hi, gain_lo, far, top, begun, out, out_top, buffer, sems):
    _, _, core, half = plan.here()
    groups = ((1 - half) * 2 + core, (1 - half) * 2 + 1 - core)
    copies = [pltpu.make_async_copy(top, out_top, sems.at[0])]
    for done, group in zip((far,), groups):
        copies.append(pltpu.make_async_copy(done, out.at[:, lanes(group, width)], sems.at[len(copies)]))
    for copy in copies:
        copy.start()
    known = split(part[...])
    step = buffer.shape[0] // 2
    for start in range(0, buffer.shape[0], step):
        rows = slice(start, start + step)
        change = dot(gain_hi[rows], known[0]) + (dot(gain_hi[rows], known[1]) + dot(gain_lo[rows], known[0]))
        buffer[rows] = base[rows, :width] - change
        copies.append(pltpu.make_async_copy(
            buffer.at[pl.ds(start, step)], out.at[pl.ds(start, step), lanes(groups[1], width)],
            sems.at[len(copies)]))
        copies[-1].start()
    for copy in copies:
        copy.wait()


def stack_place(step, level, flip):
    if level == step:
        return 2 ** (step + 1) - 2
    half = 2 ** (step - 1 - level)
    if flip < half:
        return stack_place(step - 1, level, flip)
    return 2**step - 1 + stack_place(step - 1, level, flip - half)


def top_kernel(plan, solved, back_hi, back_lo, *refs):
    levels, width = plan.levels, plan.width
    stacks, out = refs[:-1], refs[-1]
    leaf, place, _, _ = plan.here()
    second = leaf % 2 == 1
    found = {}
    for level in reversed(range(levels)):
        for flip in range(2 ** (levels - 1 - level)):
            panel = plan.panel(place, level, flip)
            if flip == 0:
                result = solved[pl.ds(level * width, width), :]
            else:
                step = flip.bit_length() - 1 + level
                number = stack_place(step, level, flip - 2 ** (step - level))
                forward = stacks[step][number]
                if step == levels - 2:
                    other = stacks[step + 1][number]
                    forward = jnp.concatenate(
                        [jnp.where(second, other, forward), jnp.where(second, forward, other)], 0)
                above = [found[up, flip >> (up - level)] for up in range(level + 1, levels)]
                result = backward(plan, back_hi, back_lo, panel, level, forward, above)
            found[level, flip] = result
            out[lanes(panel, width), :] = result


VMEM_SPEC = pl.BlockSpec(memory_space=pltpu.VMEM)
HBM_SPEC = pl.BlockSpec(memory_space=pltpu.HBM)
ANY_SPEC = pl.BlockSpec(memory_space=pl.ANY)


def call(kernel, outs, args, scratch=(), anys=(), name=None, after=(), after_hbm=(), flops=1000, alias=None):
    after_hbm = [pltpu.with_memory_space_constraint(a, pltpu.HBM) for a in after_hbm]
    after_specs = [ANY_SPEC] * len(after) + [HBM_SPEC] * len(after_hbm)
    after = list(after) + after_hbm
    count = len(args)

    def body(*refs):
        kernel(*refs[:count], *refs[count + len(after) :])

    specs = [HBM_SPEC if number in anys else VMEM_SPEC for number in range(count)]
    args = [pltpu.with_memory_space_constraint(a, pltpu.HBM if number in anys else pltpu.VMEM)
            for number, a in enumerate(args)]
    return pl.pallas_call(
        body,
        out_shape=[shape for shape, _ in outs],
        in_specs=specs + after_specs,
        out_specs=[spec for _, spec in outs],
        scratch_shapes=list(scratch),
        input_output_aliases=alias or {},
        compiler_params=pltpu.CompilerParams(vmem_limit_bytes=12 * 2**20),
        cost_estimate=pl.CostEstimate(flops=flops, bytes_accessed=1000, transcendentals=0),
        name=name,
    )(*args, *after)


def inside(shape, dtype=F32):
    return (pltpu.VMEM(shape, dtype), VMEM_SPEC)


def per_device(rhs_in, rhs_top, leaf_inv, leaf_coupling, coupling_rows, top_inv, top_coupling):
    block_count, order, _ = leaf_inv.shape
    panel_count, width, _ = top_inv.shape
    columns = rhs_top.shape[1]
    path = coupling_rows.shape[1]
    plan = Plan(lax.axis_size("leaf"), lax.axis_size("rhs"), panel_count, width)
    levels = plan.levels
    assert plan.group_count == 4 and block_count == 4 and plan.sharers >= 2

    halves = [pltpu.VMEM((order, 2 * columns), BF16)] * 2
    cut = path // 2 + 32
    pieces = [inside((cut, columns)), inside((2 * path - cut, columns))]
    sent_first, sent_second, rhs_own, lifted_other, inv_hi, inv_lo, perm_hi, perm_lo = call(
        functools.partial(lift_kernel, plan, order, columns),
        pieces + [inside((order, 2 * columns)), inside((order, 2 * columns)),
         inside((order, order), BF16), inside((order, order), BF16),
         inside((path, order), BF16), inside((path, order), BF16)],
        [rhs_in, leaf_inv, leaf_coupling, coupling_rows],
        scratch=[pltpu.VMEM((order, 2 * columns), F32), pltpu.VMEM((order, order), F32),
                 pltpu.VMEM((path, order), F32), pltpu.VMEM((1, path), jnp.int32), *halves,
                 pltpu.SemaphoreType.DMA((7,))],
        anys=(0, 1, 2, 3), name="lift")
    came_first, came_second = plan.swap_rhs(sent_first, 1), plan.swap_rhs(sent_second, 1)
    first, second, lifted_own = call(
        functools.partial(own_kernel, plan),
        pieces + [inside((order, 2 * columns))],
        [rhs_own, inv_hi, inv_lo, perm_hi, perm_lo, rhs_top], scratch=halves, name="own")
    sent = [first + came_first, second[: path - cut] + came_second[: path - cut]]
    near = second[path - cut :] + came_second[path - cut :]
    base_own, base_other, gain_hi, gain_lo, token = call(
        turn_kernel,
        [inside((order, 2 * columns)), inside((order, 2 * columns)),
         inside((order, path), BF16), inside((order, path), BF16), inside((8, columns))],
        [inv_hi, inv_lo, perm_hi, perm_lo, lifted_own, lifted_other], name="turn", after=sent)
    came = [plan.swap_rhs(part, 2) for part in sent]
    values = [near[rows] + part + token[:1] for rows, part in zip((slice(0, cut), slice(cut, path)), came)]
    fores, backs = (panel_count, levels * width, width), (panel_count, width, levels * width)
    fore_hi, fore_lo, back_hi, back_lo = call(
        ready_kernel,
        [inside(fores, BF16), inside(fores, BF16), inside(backs, BF16), inside(backs, BF16)],
        [top_inv, top_coupling], name="ready", after=values[1:])
    bit = 1
    while bit < plan.sharers // 2:
        values = [value + plan.swap_leaf(value, bit) for value in values]
        bit *= 2
    came = [plan.swap_leaf(value, bit) for value in values]
    value, came = values, came

    forwards, stacks, known = [], [], []
    for level in range(levels - 1):
        forward, rest = call(
            functools.partial(climb_kernel, plan, level, len(value)),
            [inside((width, columns)), inside(((levels - 1 - level) * width, columns))],
            value + came + [fore_hi, fore_lo], name="climb")
        bit = plan.sharers * 2**level
        value, came = [rest], [plan.swap_leaf(rest, bit)]
        forwards.append(forward)
        known = known + stacks[-1:] + [forward[None]]
        if level == levels - 2:
            stack = call(
                functools.partial(halve_kernel, plan),
                [inside((2 ** (level + 1) - 1, width // 2, columns))], known, name="halve", after=[rest])[0]
        else:
            stack = jnp.concatenate(known, 0)
        stacks.append(plan.swap_leaf(stack, bit))
    solved = call(
        functools.partial(descend_kernel, plan),
        [inside((path, columns))],
        value + came + [fore_hi, fore_lo, back_hi, back_lo] + forwards, name="descend", after=stacks[:-1])[0]

    far = plan.swap_rhs(solved, 2)

    def settle(part, base, column):
        return call(
            functools.partial(settle_kernel, columns, column),
            [inside((order, columns)), inside((8, columns))],
            [part, base, gain_hi, gain_lo], name="settle")

    own, token = settle(solved, base_own, columns)
    cross = plan.swap_rhs(solved + token[:1], 1)
    stacks.append(plan.swap_leaf(stacks[-1] + token[:1], 1))
    whole = (order, plan.group_count * columns)
    out, token = call(
        functools.partial(cross_kernel, plan, columns, columns),
        [(pltpu.HBM(whole, F32), HBM_SPEC), inside((8, columns))],
        [cross, base_other, gain_hi, gain_lo, own],
        scratch=[pltpu.VMEM((order, columns), F32), pltpu.SemaphoreType.DMA((2,))], name="cross")
    far = far + token[:1]
    last = plan.swap_rhs(far, 1)
    far, token = settle(far, base_own, 0)
    top = call(
        functools.partial(top_kernel, plan),
        [inside((panel_count * width, columns))],
        [solved, back_hi, back_lo] + stacks, name="top", after=[token], flops=5 * 10**9)[0]
    out, top = call(
        functools.partial(last_kernel, plan, columns),
        [(pltpu.HBM(whole, F32), HBM_SPEC),
         (pltpu.HBM((panel_count * width, columns), F32), HBM_SPEC)],
        [last, base_other, gain_hi, gain_lo, far, top, out], anys=(6,), alias={6: 0},
        scratch=[pltpu.VMEM((order, columns), F32), pltpu.SemaphoreType.DMA((4,))], name="last")
    return out, top


def solution(mesh):
    placed = (
        P(("leaf", "rhs"), None),
        P(None, "rhs"),
        P("leaf", None, None),
        P("leaf", None, None),
        P("leaf", None),
        P(),
        P(),
    )
    return jax.shard_map(
        per_device,
        mesh=mesh,
        in_specs=placed,
        out_specs=(P(("leaf", "rhs"), None), P(None, "rhs")),
        check_vma=False,
    )
```

```python
import functools

import jax
import jax.numpy as jnp
from jax import lax
from jax.experimental import pallas as pl
from jax.experimental.pallas import tpu as pltpu
from jax.sharding import PartitionSpec as P

F32, BF16 = jnp.float32, jnp.bfloat16
high = lax.Precision.HIGH


def dot(left, right):
    return jnp.dot(left, right, preferred_element_type=F32)


def dot_high(left, right):
    return jnp.dot(left, right, precision=high, preferred_element_type=F32)


def split(value):
    hi = value.astype(BF16)
    return hi, (value - hi.astype(F32)).astype(BF16)


def dot_split(left_hi, left_lo, right):
    hi, lo = split(right)
    return dot(left_hi, hi) + (dot(left_hi, lo) + dot(left_lo, hi))


def lanes(number, width):
    return pl.ds(pl.multiple_of(number * width, width), width)


class Plan:
    def __init__(self, leaf_count, group_count, panel_count, width):
        self.width = width
        self.levels = (panel_count + 1).bit_length() - 1
        self.bottoms = 2 ** (self.levels - 1)
        self.leaf_count, self.group_count = leaf_count, group_count
        self.sharers = leaf_count // self.bottoms

    def here(self):
        leaf, group = lax.axis_index("leaf"), lax.axis_index("rhs")
        return leaf, leaf // self.sharers, group % 2, group // 2

    def panel(self, place, level, flip=0):
        depth = self.levels - 1 - level
        return 2**depth - 1 + ((place >> level) ^ flip)

    def swap(self, value, partner):
        pairs = []
        for leaf in range(self.leaf_count):
            for group in range(self.group_count):
                to_leaf, to_group = partner(leaf, group)
                pairs.append((leaf * self.group_count + group, to_leaf * self.group_count + to_group))
        return lax.ppermute(value, ("leaf", "rhs"), pairs)

    def swap_rhs(self, value, bit):
        return self.swap(value, lambda leaf, group: (leaf, group ^ bit))

    def swap_leaf(self, value, bit):
        return self.swap(value, lambda leaf, group: (leaf ^ bit, group))


def lift_and_couple(rhs_hi, rhs_lo, inv_hi, inv_lo, perm_hi, perm_lo, lifted, first, second, hi_buf, lo_buf, step):
    path, width = perm_hi.shape[0], first.shape[1]
    cut = first.shape[0]
    for start in range(0, lifted.shape[0], step):
        rows = slice(start, start + step)
        part = dot(inv_hi[rows], rhs_hi) + (dot(inv_hi[rows], rhs_lo) + dot(inv_lo[rows], rhs_hi))
        lifted[rows] = part
        hi_buf[rows], lo_buf[rows] = split(part)
    step = path // 2
    for start in range(0, path, step):
        rows = slice(start, start + step)
        part = dot(perm_hi[rows], hi_buf[...]) + (
            dot(perm_hi[rows], lo_buf[...]) + dot(perm_lo[rows], hi_buf[...]))
        if start < cut:
            first[start : min(start + step, cut)] = -part[: min(step, cut - start), :width]
        if start + step > cut:
            skip = max(cut - start, 0)
            second[start + skip - cut : start + step - cut] = -part[skip:, :width]
        second[path - cut + start : path - cut + start + step] = -part[:, width:]


def lift_kernel(plan, order, width, rhs, inv, coupling, rows, first, second, rhs_own, lifted, inv_hi, inv_lo,
                perm_hi, perm_lo, rhs_buf, inv_buf, coup_buf, row_buf, hi_buf, lo_buf, sems):
    _, _, core, half = plan.here()
    block = half * 2 + core
    path = coupling.shape[1]
    copies = [
        pltpu.make_async_copy(rows.at[pl.ds(block, 1)], row_buf, sems.at[0]),
        pltpu.make_async_copy(coupling.at[block], coup_buf, sems.at[1]),
    ]
    for number, side in enumerate((1 - half, half)):
        copies.append(pltpu.make_async_copy(
            rhs.at[:, lanes(side * 2 + 1 - core, width)],
            rhs_buf.at[:, pl.ds(number * width, width)], sems.at[2 + number]))
    copies.append(pltpu.make_async_copy(inv.at[block], inv_buf, sems.at[4]))
    for number, side in enumerate((1 - half, half)):
        copies.append(pltpu.make_async_copy(
            rhs.at[:, lanes(side * 2 + core, width)],
            rhs_own.at[:, pl.ds(number * width, width)], sems.at[5 + number]))
    for copy in copies:
        copy.start()
    copies[0].wait()
    chosen = (lax.broadcasted_iota(jnp.int32, (path, path), 0) == row_buf[...]).astype(BF16)
    copies[1].wait()
    coup_hi, coup_lo = split(coup_buf[...])
    perm_hi[...] = dot(chosen, coup_hi).astype(BF16)
    perm_lo[...] = dot(chosen, coup_lo).astype(BF16)
    copies[2].wait()
    copies[3].wait()
    rhs_hi, rhs_lo = split(rhs_buf[...])
    copies[4].wait()
    inv_hi[...], inv_lo[...] = split(inv_buf[...])
    lift_and_couple(rhs_hi, rhs_lo, inv_hi, inv_lo, perm_hi, perm_lo, lifted, first, second, hi_buf, lo_buf,
                    order // 4)
    copies[5].wait()
    copies[6].wait()


def own_kernel(plan, rhs_own, inv_hi, inv_lo, perm_hi, perm_lo, top, first, second, lifted, hi_buf, lo_buf):
    leaf, place, _, _ = plan.here()
    rhs_hi, rhs_lo = split(rhs_own[...])
    lift_and_couple(rhs_hi, rhs_lo, inv_hi, inv_lo, perm_hi, perm_lo, lifted, first, second, hi_buf, lo_buf,
                    lifted.shape[0] // 2)
    for level in range(plan.levels):
        @pl.when(leaf % (plan.sharers * 2**level) == 0)
        def _():
            start = perm_hi.shape[0] - first.shape[0] + level * plan.width
            second[start : start + plan.width] += top[lanes(plan.panel(place, level), plan.width), :]


def ready_kernel(top_inv, top_coup, fore_hi, fore_lo, back_hi, back_lo):
    width = top_inv.shape[1]
    first = 0
    for number in range(top_inv.shape[0]):
        depth = (number + 1).bit_length() - 1
        inv = top_inv[number]
        turned = inv.T
        fore_hi[number, :width], fore_lo[number, :width] = split(inv)
        back_hi[number, :, :width], back_lo[number, :, :width] = split(turned)
        for step in range(depth):
            change = dot_high(top_coup[first + step], inv)
            place = pl.ds((step + 1) * width, width)
            fore_hi[number, place], fore_lo[number, place] = split(change)
            back_hi[number, :, place], back_lo[number, :, place] = split(-change.T)
        first += depth


def turn_kernel(inv_hi, inv_lo, perm_hi, perm_lo, lifted_own, lifted_other, base_own, base_other, gain_hi, gain_lo, token):
    hi, lo = inv_hi[...].T, inv_lo[...].T
    turned_hi, turned_lo = perm_hi[...].T, perm_lo[...].T
    gain = dot(hi, turned_hi) + (dot(hi, turned_lo) + dot(lo, turned_hi))
    gain_hi[...], gain_lo[...] = split(gain)
    base_own[...] = dot_split(hi, lo, lifted_own[...])
    base_other[...] = dot_split(hi, lo, lifted_other[...])
    token[...] = jnp.zeros_like(token)


def climb_kernel(plan, level, count, *refs):
    _, place, _, _ = plan.here()
    width = plan.width
    above = plan.levels - 1 - level
    fore_hi, fore_lo, forward, rest = refs[2 * count :]
    parts = [value[...] + came[...] for value, came in zip(refs[:count], refs[count : 2 * count])]
    total = jnp.concatenate(parts, 0) if count > 1 else parts[0]
    panel = plan.panel(place, level)
    result = dot_split(
        fore_hi[panel, : (above + 1) * width], fore_lo[panel, : (above + 1) * width], total[:width])
    forward[...] = result[:width]
    rest[...] = total[width:] - result[width:]


def backward(plan, back_hi, back_lo, panel, level, forward, above):
    depth = plan.width * (plan.levels - level)
    known = jnp.concatenate([forward] + above, 0) if above else forward
    return dot_split(back_hi[panel, :, :depth], back_lo[panel, :, :depth], known)


def halve_kernel(plan, *refs):
    leaf, _, _, _ = plan.here()
    out, number = refs[-1], 0
    for ref in refs[:-1]:
        for panel in range(ref.shape[0]):
            out[number] = ref[panel, lanes(leaf % 2, plan.width // 2), :]
            number += 1


def descend_kernel(plan, *refs):
    levels, width = plan.levels, plan.width
    value, came, fore_hi, fore_lo, back_hi, back_lo = refs[:6]
    forwards = refs[6 : 6 + levels - 1]
    solved = refs[6 + levels - 1]
    _, place, _, _ = plan.here()
    panels = [plan.panel(place, level) for level in range(levels)]

    def part(level, step, known):
        columns = slice(step * width, (step + 1) * width)
        return dot_split(back_hi[panels[level], :, columns], back_lo[panels[level], :, columns], known)

    totals = [part(level, 0, forwards[level][...]) for level in range(levels - 1)]
    top = dot_split(fore_hi[0, :width], fore_lo[0, :width], value[...] + came[...])
    totals.append(part(levels - 1, 0, top))
    for above in reversed(range(levels)):
        solved[pl.ds(above * width, width), :] = totals[above]
        for level in reversed(range(above)):
            totals[level] = totals[level] + part(level, above - level, totals[above])


def settled(base, gain_hi, gain_lo, part, column, width):
    change = dot_split(gain_hi[...], gain_lo[...], part[...])
    return base[:, column : column + width] - change


def settle_kernel(width, column, part, base, gain_hi, gain_lo, out, token):
    out[...] = settled(base, gain_hi, gain_lo, part, column, width)
    token[...] = jnp.zeros_like(token)


def cross_kernel(plan, width, column, part, base, gain_hi, gain_lo, own, out, token, buffer, sems):
    _, _, core, half = plan.here()
    copies = [pltpu.make_async_copy(own, out.at[:, lanes(half * 2 + core, width)], sems.at[0]),
              pltpu.make_async_copy(buffer, out.at[:, lanes(half * 2 + 1 - core, width)], sems.at[1])]
    copies[0].start()
    buffer[...] = settled(base, gain_hi, gain_lo, part, column, width)
    copies[1].start()
    token[...] = jnp.zeros_like(token)
    for copy in copies:
        copy.wait()


def last_kernel(plan, width, part, base, gain_hi, gain_lo, far, top, begun, out, out_top, buffer, sems):
    _, _, core, half = plan.here()
    groups = ((1 - half) * 2 + core, (1 - half) * 2 + 1 - core)
    copies = [pltpu.make_async_copy(top, out_top, sems.at[0])]
    for done, group in zip((far,), groups):
        copies.append(pltpu.make_async_copy(done, out.at[:, lanes(group, width)], sems.at[len(copies)]))
    for copy in copies:
        copy.start()
    known = split(part[...])
    step = buffer.shape[0] // 2
    for start in range(0, buffer.shape[0], step):
        rows = slice(start, start + step)
        change = dot(gain_hi[rows], known[0]) + (dot(gain_hi[rows], known[1]) + dot(gain_lo[rows], known[0]))
        buffer[rows] = base[rows, :width] - change
        copies.append(pltpu.make_async_copy(
            buffer.at[pl.ds(start, step)], out.at[pl.ds(start, step), lanes(groups[1], width)],
            sems.at[len(copies)]))
        copies[-1].start()
    for copy in copies:
        copy.wait()


def stack_place(step, level, flip):
    if level == step:
        return 2 ** (step + 1) - 2
    half = 2 ** (step - 1 - level)
    if flip < half:
        return stack_place(step - 1, level, flip)
    return 2**step - 1 + stack_place(step - 1, level, flip - half)


def top_kernel(plan, solved, back_hi, back_lo, *refs):
    levels, width = plan.levels, plan.width
    stacks, out = refs[:-1], refs[-1]
    leaf, place, _, _ = plan.here()
    second = leaf % 2 == 1
    found = {}
    for level in reversed(range(levels)):
        for flip in range(2 ** (levels - 1 - level)):
            panel = plan.panel(place, level, flip)
            if flip == 0:
                result = solved[pl.ds(level * width, width), :]
            else:
                step = flip.bit_length() - 1 + level
                number = stack_place(step, level, flip - 2 ** (step - level))
                forward = stacks[step][number]
                if step == levels - 2:
                    other = stacks[step + 1][number]
                    forward = jnp.concatenate(
                        [jnp.where(second, other, forward), jnp.where(second, forward, other)], 0)
                above = [found[up, flip >> (up - level)] for up in range(level + 1, levels)]
                result = backward(plan, back_hi, back_lo, panel, level, forward, above)
            found[level, flip] = result
            out[lanes(panel, width), :] = result


VMEM_SPEC = pl.BlockSpec(memory_space=pltpu.VMEM)
HBM_SPEC = pl.BlockSpec(memory_space=pltpu.HBM)
ANY_SPEC = pl.BlockSpec(memory_space=pl.ANY)


def call(kernel, outs, args, scratch=(), anys=(), name=None, after=(), after_hbm=(), flops=1000, alias=None):
    after_hbm = [pltpu.with_memory_space_constraint(a, pltpu.HBM) for a in after_hbm]
    after_specs = [ANY_SPEC] * len(after) + [HBM_SPEC] * len(after_hbm)
    after = list(after) + after_hbm
    count = len(args)

    def body(*refs):
        kernel(*refs[:count], *refs[count + len(after) :])

    specs = [HBM_SPEC if number in anys else VMEM_SPEC for number in range(count)]
    args = [pltpu.with_memory_space_constraint(a, pltpu.HBM if number in anys else pltpu.VMEM)
            for number, a in enumerate(args)]
    return pl.pallas_call(
        body,
        out_shape=[shape for shape, _ in outs],
        in_specs=specs + after_specs,
        out_specs=[spec for _, spec in outs],
        scratch_shapes=list(scratch),
        input_output_aliases=alias or {},
        compiler_params=pltpu.CompilerParams(vmem_limit_bytes=12 * 2**20),
        cost_estimate=pl.CostEstimate(flops=flops, bytes_accessed=1000, transcendentals=0),
        name=name,
    )(*args, *after)


def inside(shape, dtype=F32):
    return (pltpu.VMEM(shape, dtype), VMEM_SPEC)


def per_device(rhs_in, rhs_top, leaf_inv, leaf_coupling, coupling_rows, top_inv, top_coupling):
    block_count, order, _ = leaf_inv.shape
    panel_count, width, _ = top_inv.shape
    columns = rhs_top.shape[1]
    path = coupling_rows.shape[1]
    plan = Plan(lax.axis_size("leaf"), lax.axis_size("rhs"), panel_count, width)
    levels = plan.levels
    assert plan.group_count == 4 and block_count == 4 and plan.sharers >= 2

    halves = [pltpu.VMEM((order, 2 * columns), BF16)] * 2
    cut = path // 2 + 32
    pieces = [inside((cut, columns)), inside((2 * path - cut, columns))]
    sent_first, sent_second, rhs_own, lifted_other, inv_hi, inv_lo, perm_hi, perm_lo = call(
        functools.partial(lift_kernel, plan, order, columns),
        pieces + [inside((order, 2 * columns)), inside((order, 2 * columns)),
         inside((order, order), BF16), inside((order, order), BF16),
         inside((path, order), BF16), inside((path, order), BF16)],
        [rhs_in, leaf_inv, leaf_coupling, coupling_rows],
        scratch=[pltpu.VMEM((order, 2 * columns), F32), pltpu.VMEM((order, order), F32),
                 pltpu.VMEM((path, order), F32), pltpu.VMEM((1, path), jnp.int32), *halves,
                 pltpu.SemaphoreType.DMA((7,))],
        anys=(0, 1, 2, 3), name="lift")
    came_first, came_second = plan.swap_rhs(sent_first, 1), plan.swap_rhs(sent_second, 1)
    first, second, lifted_own = call(
        functools.partial(own_kernel, plan),
        pieces + [inside((order, 2 * columns))],
        [rhs_own, inv_hi, inv_lo, perm_hi, perm_lo, rhs_top], scratch=halves, name="own")
    sent = [first + came_first, second[: path - cut] + came_second[: path - cut]]
    near = second[path - cut :] + came_second[path - cut :]
    base_own, base_other, gain_hi, gain_lo, token = call(
        turn_kernel,
        [inside((order, 2 * columns)), inside((order, 2 * columns)),
         inside((order, path), BF16), inside((order, path), BF16), inside((8, columns))],
        [inv_hi, inv_lo, perm_hi, perm_lo, lifted_own, lifted_other], name="turn", after=sent)
    came = [plan.swap_rhs(part, 2) for part in sent]
    values = [near[rows] + part + token[:1] for rows, part in zip((slice(0, cut), slice(cut, path)), came)]
    fores, backs = (panel_count, levels * width, width), (panel_count, width, levels * width)
    fore_hi, fore_lo, back_hi, back_lo = call(
        ready_kernel,
        [inside(fores, BF16), inside(fores, BF16), inside(backs, BF16), inside(backs, BF16)],
        [top_inv, top_coupling], name="ready", after=values[1:])
    bit = 1
    while bit < plan.sharers // 2:
        values = [value + plan.swap_leaf(value, bit) for value in values]
        bit *= 2
    came = [plan.swap_leaf(value, bit) for value in values]
    value, came = values, came

    forwards, stacks, known = [], [], []
    for level in range(levels - 1):
        forward, rest = call(
            functools.partial(climb_kernel, plan, level, len(value)),
            [inside((width, columns)), inside(((levels - 1 - level) * width, columns))],
            value + came + [fore_hi, fore_lo], name="climb")
        bit = plan.sharers * 2**level
        value, came = [rest], [plan.swap_leaf(rest, bit)]
        forwards.append(forward)
        known = known + stacks[-1:] + [forward[None]]
        if level == levels - 2:
            stack = call(
                functools.partial(halve_kernel, plan),
                [inside((2 ** (level + 1) - 1, width // 2, columns))], known, name="halve", after=[rest])[0]
        else:
            stack = jnp.concatenate(known, 0)
        stacks.append(plan.swap_leaf(stack, bit))
    solved = call(
        functools.partial(descend_kernel, plan),
        [inside((path, columns))],
        value + came + [fore_hi, fore_lo, back_hi, back_lo] + forwards, name="descend", after=stacks[:-1])[0]

    far = plan.swap_rhs(solved, 2)

    def settle(part, base, column):
        return call(
            functools.partial(settle_kernel, columns, column),
            [inside((order, columns)), inside((8, columns))],
            [part, base, gain_hi, gain_lo], name="settle")

    own, token = settle(solved, base_own, columns)
    cross = plan.swap_rhs(solved + token[:1], 1)
    stacks.append(plan.swap_leaf(stacks[-1] + token[:1], 1))
    whole = (order, plan.group_count * columns)
    out, token = call(
        functools.partial(cross_kernel, plan, columns, columns),
        [(pltpu.HBM(whole, F32), HBM_SPEC), inside((8, columns))],
        [cross, base_other, gain_hi, gain_lo, own],
        scratch=[pltpu.VMEM((order, columns), F32), pltpu.SemaphoreType.DMA((2,))], name="cross")
    far = far + token[:1]
    last = plan.swap_rhs(far, 1)
    far, token = settle(far, base_own, 0)
    top = call(
        functools.partial(top_kernel, plan),
        [inside((panel_count * width, columns))],
        [solved, back_hi, back_lo] + stacks, name="top", after=[token], flops=5 * 10**9)[0]
    out, top = call(
        functools.partial(last_kernel, plan, columns),
        [(pltpu.HBM(whole, F32), HBM_SPEC),
         (pltpu.HBM((panel_count * width, columns), F32), HBM_SPEC)],
        [last, base_other, gain_hi, gain_lo, far, top, out], anys=(6,), alias={6: 0},
        scratch=[pltpu.VMEM((order, columns), F32), pltpu.SemaphoreType.DMA((4,))], name="last")
    return out, top


def solution(mesh):
    placed = (
        P(("leaf", "rhs"), None),
        P(None, "rhs"),
        P("leaf", None, None),
        P("leaf", None, None),
        P("leaf", None),
        P(),
        P(),
    )
    return jax.shard_map(
        per_device,
        mesh=mesh,
        in_specs=placed,
        out_specs=(P(("leaf", "rhs"), None), P(None, "rhs")),
        check_vma=False,
    )
```

```python
import functools

import jax
import jax.numpy as jnp
from jax import lax
from jax.experimental import pallas as pl
from jax.experimental.pallas import tpu as pltpu
from jax.sharding import PartitionSpec as P

F32, BF16 = jnp.float32, jnp.bfloat16
high = lax.Precision.HIGH


def dot(left, right):
    return jnp.dot(left, right, preferred_element_type=F32)


def dot_high(left, right):
    return jnp.dot(left, right, precision=high, preferred_element_type=F32)


def split(value):
    hi = value.astype(BF16)
    return hi, (value - hi.astype(F32)).astype(BF16)


def dot_split(left_hi, left_lo, right):
    hi, lo = split(right)
    return dot(left_hi, hi) + (dot(left_hi, lo) + dot(left_lo, hi))


def lanes(number, width):
    return pl.ds(pl.multiple_of(number * width, width), width)


class Plan:
    def __init__(self, leaf_count, group_count, panel_count, width):
        self.width = width
        self.levels = (panel_count + 1).bit_length() - 1
        self.bottoms = 2 ** (self.levels - 1)
        self.leaf_count, self.group_count = leaf_count, group_count
        self.sharers = leaf_count // self.bottoms

    def here(self):
        leaf, group = lax.axis_index("leaf"), lax.axis_index("rhs")
        return leaf, leaf // self.sharers, group % 2, group // 2

    def panel(self, place, level, flip=0):
        depth = self.levels - 1 - level
        return 2**depth - 1 + ((place >> level) ^ flip)

    def swap(self, value, partner):
        pairs = []
        for leaf in range(self.leaf_count):
            for group in range(self.group_count):
                to_leaf, to_group = partner(leaf, group)
                pairs.append((leaf * self.group_count + group, to_leaf * self.group_count + to_group))
        return lax.ppermute(value, ("leaf", "rhs"), pairs)

    def swap_rhs(self, value, bit):
        return self.swap(value, lambda leaf, group: (leaf, group ^ bit))

    def swap_leaf(self, value, bit):
        return self.swap(value, lambda leaf, group: (leaf ^ bit, group))


def lift_and_couple(rhs_hi, rhs_lo, inv_hi, inv_lo, perm_hi, perm_lo, lifted, first, second, hi_buf, lo_buf, step):
    path, width = perm_hi.shape[0], first.shape[1]
    cut = first.shape[0]
    for start in range(0, lifted.shape[0], step):
        rows = slice(start, start + step)
        part = dot(inv_hi[rows], rhs_hi) + (dot(inv_hi[rows], rhs_lo) + dot(inv_lo[rows], rhs_hi))
        lifted[rows] = part
        hi_buf[rows], lo_buf[rows] = split(part)
    step = path // 2
    for start in range(0, path, step):
        rows = slice(start, start + step)
        part = dot(perm_hi[rows], hi_buf[...]) + (
            dot(perm_hi[rows], lo_buf[...]) + dot(perm_lo[rows], hi_buf[...]))
        if start < cut:
            first[start : min(start + step, cut)] = -part[: min(step, cut - start), :width]
        if start + step > cut:
            skip = max(cut - start, 0)
            second[start + skip - cut : start + step - cut] = -part[skip:, :width]
        second[path - cut + start : path - cut + start + step] = -part[:, width:]


def lift_kernel(plan, order, width, rhs, inv, coupling, rows, first, second, rhs_own, lifted, inv_hi, inv_lo,
                perm_hi, perm_lo, rhs_buf, inv_buf, coup_buf, row_buf, hi_buf, lo_buf, sems):
    _, _, core, half = plan.here()
    block = half * 2 + core
    path = coupling.shape[1]
    copies = [
        pltpu.make_async_copy(rows.at[pl.ds(block, 1)], row_buf, sems.at[0]),
        pltpu.make_async_copy(coupling.at[block], coup_buf, sems.at[1]),
    ]
    for number, side in enumerate((1 - half, half)):
        copies.append(pltpu.make_async_copy(
            rhs.at[:, lanes(side * 2 + 1 - core, width)],
            rhs_buf.at[:, pl.ds(number * width, width)], sems.at[2 + number]))
    copies.append(pltpu.make_async_copy(inv.at[block], inv_buf, sems.at[4]))
    for number, side in enumerate((1 - half, half)):
        copies.append(pltpu.make_async_copy(
            rhs.at[:, lanes(side * 2 + core, width)],
            rhs_own.at[:, pl.ds(number * width, width)], sems.at[5 + number]))
    for copy in copies:
        copy.start()
    copies[0].wait()
    chosen = (lax.broadcasted_iota(jnp.int32, (path, path), 0) == row_buf[...]).astype(BF16)
    copies[1].wait()
    coup_hi, coup_lo = split(coup_buf[...])
    perm_hi[...] = dot(chosen, coup_hi).astype(BF16)
    perm_lo[...] = dot(chosen, coup_lo).astype(BF16)
    copies[2].wait()
    copies[3].wait()
    rhs_hi, rhs_lo = split(rhs_buf[...])
    copies[4].wait()
    inv_hi[...], inv_lo[...] = split(inv_buf[...])
    lift_and_couple(rhs_hi, rhs_lo, inv_hi, inv_lo, perm_hi, perm_lo, lifted, first, second, hi_buf, lo_buf,
                    order // 4)
    copies[5].wait()
    copies[6].wait()


def own_kernel(plan, rhs_own, inv_hi, inv_lo, perm_hi, perm_lo, top, first, second, lifted, hi_buf, lo_buf):
    leaf, place, _, _ = plan.here()
    rhs_hi, rhs_lo = split(rhs_own[...])
    lift_and_couple(rhs_hi, rhs_lo, inv_hi, inv_lo, perm_hi, perm_lo, lifted, first, second, hi_buf, lo_buf,
                    lifted.shape[0] // 2)
    for level in range(plan.levels):
        @pl.when(leaf % (plan.sharers * 2**level) == 0)
        def _():
            start = perm_hi.shape[0] - first.shape[0] + level * plan.width
            second[start : start + plan.width] += top[lanes(plan.panel(place, level), plan.width), :]


def ready_kernel(top_inv, top_coup, fore_hi, fore_lo, back_hi, back_lo):
    width = top_inv.shape[1]
    first = 0
    for number in range(top_inv.shape[0]):
        depth = (number + 1).bit_length() - 1
        inv = top_inv[number]
        turned = inv.T
        fore_hi[number, :width], fore_lo[number, :width] = split(inv)
        back_hi[number, :, :width], back_lo[number, :, :width] = split(turned)
        for step in range(depth):
            change = dot_high(top_coup[first + step], inv)
            place = pl.ds((step + 1) * width, width)
            fore_hi[number, place], fore_lo[number, place] = split(change)
            back_hi[number, :, place], back_lo[number, :, place] = split(-change.T)
        first += depth


def turn_kernel(inv_hi, inv_lo, perm_hi, perm_lo, lifted_own, lifted_other, base_own, base_other, gain_hi, gain_lo, token):
    hi, lo = inv_hi[...].T, inv_lo[...].T
    turned_hi, turned_lo = perm_hi[...].T, perm_lo[...].T
    gain = dot(hi, turned_hi) + (dot(hi, turned_lo) + dot(lo, turned_hi))
    gain_hi[...], gain_lo[...] = split(gain)
    base_own[...] = dot_split(hi, lo, lifted_own[...])
    base_other[...] = dot_split(hi, lo, lifted_other[...])
    token[...] = jnp.zeros_like(token)


def climb_kernel(plan, level, count, *refs):
    _, place, _, _ = plan.here()
    width = plan.width
    above = plan.levels - 1 - level
    fore_hi, fore_lo, forward, rest = refs[2 * count :]
    parts = [value[...] + came[...] for value, came in zip(refs[:count], refs[count : 2 * count])]
    total = jnp.concatenate(parts, 0) if count > 1 else parts[0]
    panel = plan.panel(place, level)
    result = dot_split(
        fore_hi[panel, : (above + 1) * width], fore_lo[panel, : (above + 1) * width], total[:width])
    forward[...] = result[:width]
    rest[...] = total[width:] - result[width:]


def backward(plan, back_hi, back_lo, panel, level, forward, above):
    depth = plan.width * (plan.levels - level)
    known = jnp.concatenate([forward] + above, 0) if above else forward
    return dot_split(back_hi[panel, :, :depth], back_lo[panel, :, :depth], known)


def halve_kernel(plan, *refs):
    leaf, _, _, _ = plan.here()
    out, number = refs[-1], 0
    for ref in refs[:-1]:
        for panel in range(ref.shape[0]):
            out[number] = ref[panel, lanes(leaf % 2, plan.width // 2), :]
            number += 1


def descend_kernel(plan, *refs):
    levels, width = plan.levels, plan.width
    value, came, fore_hi, fore_lo, back_hi, back_lo = refs[:6]
    forwards = refs[6 : 6 + levels - 1]
    solved = refs[6 + levels - 1]
    _, place, _, _ = plan.here()
    top = dot_split(fore_hi[0, :width], fore_lo[0, :width], value[...] + came[...])
    above = []
    for level in reversed(range(levels)):
        forward = top if level == levels - 1 else forwards[level][...]
        result = backward(plan, back_hi, back_lo, plan.panel(place, level), level, forward, above)
        solved[pl.ds(level * width, width), :] = result
        above = [result] + above


def settled(base, gain_hi, gain_lo, part, column, width):
    change = dot_split(gain_hi[...], gain_lo[...], part[...])
    return base[:, column : column + width] - change


def settle_kernel(width, column, part, base, gain_hi, gain_lo, out, token):
    out[...] = settled(base, gain_hi, gain_lo, part, column, width)
    token[...] = jnp.zeros_like(token)


def cross_kernel(plan, width, column, part, base, gain_hi, gain_lo, own, out, token, buffer, sems):
    _, _, core, half = plan.here()
    copies = [pltpu.make_async_copy(own, out.at[:, lanes(half * 2 + core, width)], sems.at[0]),
              pltpu.make_async_copy(buffer, out.at[:, lanes(half * 2 + 1 - core, width)], sems.at[1])]
    copies[0].start()
    buffer[...] = settled(base, gain_hi, gain_lo, part, column, width)
    copies[1].start()
    token[...] = jnp.zeros_like(token)
    for copy in copies:
        copy.wait()


def last_kernel(plan, width, part, base, gain_hi, gain_lo, far, top, begun, out, out_top, buffer, sems):
    _, _, core, half = plan.here()
    groups = ((1 - half) * 2 + core, (1 - half) * 2 + 1 - core)
    copies = [pltpu.make_async_copy(top, out_top, sems.at[0])]
    for done, group in zip((far,), groups):
        copies.append(pltpu.make_async_copy(done, out.at[:, lanes(group, width)], sems.at[len(copies)]))
    for copy in copies:
        copy.start()
    known = split(part[...])
    step = buffer.shape[0] // 4
    for start in range(0, buffer.shape[0], step):
        rows = slice(start, start + step)
        change = dot(gain_hi[rows], known[0]) + (dot(gain_hi[rows], known[1]) + dot(gain_lo[rows], known[0]))
        buffer[rows] = base[rows, :width] - change
        copies.append(pltpu.make_async_copy(
            buffer.at[pl.ds(start, step)], out.at[pl.ds(start, step), lanes(groups[1], width)],
            sems.at[len(copies)]))
        copies[-1].start()
    for copy in copies:
        copy.wait()


def stack_place(step, level, flip):
    if level == step:
        return 2 ** (step + 1) - 2
    half = 2 ** (step - 1 - level)
    if flip < half:
        return stack_place(step - 1, level, flip)
    return 2**step - 1 + stack_place(step - 1, level, flip - half)


def top_kernel(plan, solved, back_hi, back_lo, *refs):
    levels, width = plan.levels, plan.width
    stacks, out = refs[:-1], refs[-1]
    leaf, place, _, _ = plan.here()
    second = leaf % 2 == 1
    found = {}
    for level in reversed(range(levels)):
        for flip in range(2 ** (levels - 1 - level)):
            panel = plan.panel(place, level, flip)
            if flip == 0:
                result = solved[pl.ds(level * width, width), :]
            else:
                step = flip.bit_length() - 1 + level
                number = stack_place(step, level, flip - 2 ** (step - level))
                forward = stacks[step][number]
                if step == levels - 2:
                    other = stacks[step + 1][number]
                    forward = jnp.concatenate(
                        [jnp.where(second, other, forward), jnp.where(second, forward, other)], 0)
                above = [found[up, flip >> (up - level)] for up in range(level + 1, levels)]
                result = backward(plan, back_hi, back_lo, panel, level, forward, above)
            found[level, flip] = result
            out[lanes(panel, width), :] = result


VMEM_SPEC = pl.BlockSpec(memory_space=pltpu.VMEM)
HBM_SPEC = pl.BlockSpec(memory_space=pltpu.HBM)
ANY_SPEC = pl.BlockSpec(memory_space=pl.ANY)


def call(kernel, outs, args, scratch=(), anys=(), name=None, after=(), after_hbm=(), flops=1000, alias=None):
    after_hbm = [pltpu.with_memory_space_constraint(a, pltpu.HBM) for a in after_hbm]
    after_specs = [ANY_SPEC] * len(after) + [HBM_SPEC] * len(after_hbm)
    after = list(after) + after_hbm
    count = len(args)

    def body(*refs):
        kernel(*refs[:count], *refs[count + len(after) :])

    specs = [HBM_SPEC if number in anys else VMEM_SPEC for number in range(count)]
    args = [pltpu.with_memory_space_constraint(a, pltpu.HBM if number in anys else pltpu.VMEM)
            for number, a in enumerate(args)]
    return pl.pallas_call(
        body,
        out_shape=[shape for shape, _ in outs],
        in_specs=specs + after_specs,
        out_specs=[spec for _, spec in outs],
        scratch_shapes=list(scratch),
        input_output_aliases=alias or {},
        compiler_params=pltpu.CompilerParams(vmem_limit_bytes=12 * 2**20),
        cost_estimate=pl.CostEstimate(flops=flops, bytes_accessed=1000, transcendentals=0),
        name=name,
    )(*args, *after)


def inside(shape, dtype=F32):
    return (pltpu.VMEM(shape, dtype), VMEM_SPEC)


def per_device(rhs_in, rhs_top, leaf_inv, leaf_coupling, coupling_rows, top_inv, top_coupling):
    block_count, order, _ = leaf_inv.shape
    panel_count, width, _ = top_inv.shape
    columns = rhs_top.shape[1]
    path = coupling_rows.shape[1]
    plan = Plan(lax.axis_size("leaf"), lax.axis_size("rhs"), panel_count, width)
    levels = plan.levels
    assert plan.group_count == 4 and block_count == 4 and plan.sharers >= 2

    halves = [pltpu.VMEM((order, 2 * columns), BF16)] * 2
    cut = path // 2 + 32
    pieces = [inside((cut, columns)), inside((2 * path - cut, columns))]
    sent_first, sent_second, rhs_own, lifted_other, inv_hi, inv_lo, perm_hi, perm_lo = call(
        functools.partial(lift_kernel, plan, order, columns),
        pieces + [inside((order, 2 * columns)), inside((order, 2 * columns)),
         inside((order, order), BF16), inside((order, order), BF16),
         inside((path, order), BF16), inside((path, order), BF16)],
        [rhs_in, leaf_inv, leaf_coupling, coupling_rows],
        scratch=[pltpu.VMEM((order, 2 * columns), F32), pltpu.VMEM((order, order), F32),
                 pltpu.VMEM((path, order), F32), pltpu.VMEM((1, path), jnp.int32), *halves,
                 pltpu.SemaphoreType.DMA((7,))],
        anys=(0, 1, 2, 3), name="lift")
    came_first, came_second = plan.swap_rhs(sent_first, 1), plan.swap_rhs(sent_second, 1)
    first, second, lifted_own = call(
        functools.partial(own_kernel, plan),
        pieces + [inside((order, 2 * columns))],
        [rhs_own, inv_hi, inv_lo, perm_hi, perm_lo, rhs_top], scratch=halves, name="own")
    sent = [first + came_first, second[: path - cut] + came_second[: path - cut]]
    near = second[path - cut :] + came_second[path - cut :]
    base_own, base_other, gain_hi, gain_lo, token = call(
        turn_kernel,
        [inside((order, 2 * columns)), inside((order, 2 * columns)),
         inside((order, path), BF16), inside((order, path), BF16), inside((8, columns))],
        [inv_hi, inv_lo, perm_hi, perm_lo, lifted_own, lifted_other], name="turn", after=sent)
    came = [plan.swap_rhs(part, 2) for part in sent]
    values = [near[rows] + part + token[:1] for rows, part in zip((slice(0, cut), slice(cut, path)), came)]
    fores, backs = (panel_count, levels * width, width), (panel_count, width, levels * width)
    fore_hi, fore_lo, back_hi, back_lo = call(
        ready_kernel,
        [inside(fores, BF16), inside(fores, BF16), inside(backs, BF16), inside(backs, BF16)],
        [top_inv, top_coupling], name="ready", after=values[1:])
    bit = 1
    while bit < plan.sharers // 2:
        values = [value + plan.swap_leaf(value, bit) for value in values]
        bit *= 2
    came = [plan.swap_leaf(value, bit) for value in values]
    value, came = values, came

    forwards, stacks, known = [], [], []
    for level in range(levels - 1):
        forward, rest = call(
            functools.partial(climb_kernel, plan, level, len(value)),
            [inside((width, columns)), inside(((levels - 1 - level) * width, columns))],
            value + came + [fore_hi, fore_lo], name="climb")
        bit = plan.sharers * 2**level
        value, came = [rest], [plan.swap_leaf(rest, bit)]
        forwards.append(forward)
        known = known + stacks[-1:] + [forward[None]]
        if level == levels - 2:
            stack = call(
                functools.partial(halve_kernel, plan),
                [inside((2 ** (level + 1) - 1, width // 2, columns))], known, name="halve", after=[rest])[0]
        else:
            stack = jnp.concatenate(known, 0)
        stacks.append(plan.swap_leaf(stack, bit))
    solved = call(
        functools.partial(descend_kernel, plan),
        [inside((path, columns))],
        value + came + [fore_hi, fore_lo, back_hi, back_lo] + forwards, name="descend", after=stacks[:-1])[0]

    far = plan.swap_rhs(solved, 2)

    def settle(part, base, column):
        return call(
            functools.partial(settle_kernel, columns, column),
            [inside((order, columns)), inside((8, columns))],
            [part, base, gain_hi, gain_lo], name="settle")

    own, token = settle(solved, base_own, columns)
    cross = plan.swap_rhs(solved + token[:1], 1)
    stacks.append(plan.swap_leaf(stacks[-1] + token[:1], 1))
    whole = (order, plan.group_count * columns)
    out, token = call(
        functools.partial(cross_kernel, plan, columns, columns),
        [(pltpu.HBM(whole, F32), HBM_SPEC), inside((8, columns))],
        [cross, base_other, gain_hi, gain_lo, own],
        scratch=[pltpu.VMEM((order, columns), F32), pltpu.SemaphoreType.DMA((2,))], name="cross")
    far = far + token[:1]
    last = plan.swap_rhs(far, 1)
    far, token = settle(far, base_own, 0)
    top = call(
        functools.partial(top_kernel, plan),
        [inside((panel_count * width, columns))],
        [solved, back_hi, back_lo] + stacks, name="top", after=[token], flops=5 * 10**9)[0]
    out, top = call(
        functools.partial(last_kernel, plan, columns),
        [(pltpu.HBM(whole, F32), HBM_SPEC),
         (pltpu.HBM((panel_count * width, columns), F32), HBM_SPEC)],
        [last, base_other, gain_hi, gain_lo, far, top, out], anys=(6,), alias={6: 0},
        scratch=[pltpu.VMEM((order, columns), F32), pltpu.SemaphoreType.DMA((6,))], name="last")
    return out, top


def solution(mesh):
    placed = (
        P(("leaf", "rhs"), None),
        P(None, "rhs"),
        P("leaf", None, None),
        P("leaf", None, None),
        P("leaf", None),
        P(),
        P(),
    )
    return jax.shard_map(
        per_device,
        mesh=mesh,
        in_specs=placed,
        out_specs=(P(("leaf", "rhs"), None), P(None, "rhs")),
        check_vma=False,
    )
```
